32 devices in a mesh: chan: 8 (over z, y), tm: 4 (over x, core).
Axes of the slice: x: 2, y: 2, z: 4, core: 2. Of those that a mesh axis runs over, the one named last changes fastest.
Arguments:
- voltages: bfloat16 [2048, 524288], P('chan', 'tm'), may hold values from -6 to 6
- taps: float32 [8, 8192], replicated, may hold values from -2 to 2
- flags: int32 [2048, 64], P('chan', 'tm'), may hold values 0 or 1
- offsets: int32 [8], P('chan'), may hold values from 0 to 7
Outputs:
- visibilities: bfloat16 [8, 2048, 2, 2048], P('chan', 'tm')
The draws below stay inside these ranges and needn't reach their ends.
All inputs are finite; a program needn't handle non-finite values. No bound on the sum of `flags` on one device may be relied on, other than what follows from the above.
Results may differ from the reference program's by a relative error of at most 0.0058.
Values may be sent and summed in bfloat16 or wider, within the bound.
No kernel may reach another device: no remote copies, remote signals or barrier semaphores. Data moves between devices by JAX's collectives and lax.ppermute only.
A program may use at most 384 MiB of HBM per device.

```python
import math
import jax
import jax.numpy as jnp
from jax import lax

INPUTS = 2048
FRAME = 8192
TAPS = 8
SPECTRA = 64
CHANNELS = 8
N_CHAN = 8


def set_ends(values, own_key, smallest, largest):
    spot = [jax.random.randint(jax.random.fold_in(own_key, axis), (), 0, length) for axis, length in enumerate(values.shape)]
    widest = values.shape.index(max(values.shape))
    beside = spot[:widest] + [(spot[widest] + 1) % values.shape[widest]] + spot[widest + 1:]
    return values.at[tuple(spot)].set(smallest).at[tuple(beside)].set(largest)


def shard_levels(rng, dims, cuts, least, top_value):
    def one(position, shards_of):
        steps = jax.random.uniform(jax.random.fold_in(jax.random.fold_in(rng, 6), position), (shards_of,), jnp.float32, least / len(cuts), top_value / len(cuts))
        return jnp.repeat(jnp.exp(steps), dims[position] // shards_of).reshape((-1,) + (1,) * (len(dims) - position - 1))

    level = one(*cuts[0])
    for cut in cuts[1:]:
        level = level * one(*cut)
    return level


def scatter_about(rng, shape, spread, most, split=(), held_as=jnp.bfloat16):
    drawn = spread * jax.random.normal(rng, shape, jnp.float32)
    if split:
        drawn = drawn * shard_levels(rng, shape, split, -0.22, 0.18)
    return jnp.clip(drawn, -most, most).astype(held_as)


def setup_inputs(seed: int = 0) -> dict:
    splits = jax.random.split(jax.random.key(seed), 5)
    return {
        "voltages": scatter_about(splits[0], (INPUTS, SPECTRA * FRAME), 1.0, 6.0, ((0, 8), (1, 4))),
        "taps": scatter_about(splits[1], (TAPS, FRAME), 0.35, 2.0, (), jnp.float32),
        "flags": set_ends((jax.random.randint(splits[2], (INPUTS, SPECTRA), 0, 8) < 7).astype(jnp.int32), jax.random.fold_in(splits[2], 1), 0, 1),
        "offsets": set_ends(jax.random.randint(splits[3], (CHANNELS,), 0, N_CHAN), jax.random.fold_in(splits[3], 1), 0, N_CHAN - 1).astype(jnp.int32),
    }


def channel_table(frame, channels, zero_shift):
    samples = jnp.arange(frame, dtype=jnp.int32) + zero_shift
    numbers = jnp.arange(channels, dtype=jnp.int32) * (frame // (2 * channels)) + frame // (4 * channels)
    phase = samples[:, None] * numbers[None, :] % frame
    angle = phase.astype(jnp.float32) * (2.0 * math.pi / frame)
    norm_scale = 1.0 / math.sqrt(frame)
    return jnp.stack([jnp.cos(angle) * norm_scale, -jnp.sin(angle) * norm_scale], axis=2)

def filter_frames(extended, taps, frame_count):
    history = taps.shape[0] - 1
    total = jnp.zeros((extended.shape[0], frame_count, extended.shape[2]), jnp.float32)
    for tap_index in range(taps.shape[0]):
        begin = history - tap_index
        total = total + taps[tap_index][None, None, :] * extended[:, begin:begin + frame_count, :].astype(jnp.float32)
    return total

def build_columns(real_part, imag_part, rotation):
    rolled_real = jnp.roll(real_part, -rotation, axis=1)
    rolled_imag = jnp.roll(imag_part, -rotation, axis=1)
    first = jnp.concatenate([rolled_real, rolled_imag], axis=0)
    second = jnp.concatenate([-rolled_imag, rolled_real], axis=0)
    return jnp.stack([first, second], axis=1)

def products(row_side, col_side):
    width = col_side.shape[2]
    flat = col_side.reshape(col_side.shape[0], 2 * width)
    result = jnp.dot(row_side.T, flat, preferred_element_type=jnp.float32)
    return result.reshape(row_side.shape[1], 2, width)

def reference(voltages, taps, flags, offsets):
    zero_shift = jnp.minimum(offsets[0], 0).astype(jnp.int32)
    dft_table = channel_table(FRAME, CHANNELS, zero_shift)
    blocks = INPUTS // N_CHAN
    volt_blocks = voltages.reshape(N_CHAN, blocks, SPECTRA, FRAME)
    flag_blocks = flags.reshape(N_CHAN, blocks, SPECTRA)

    def filter_block(pair):
        volt, flag = pair
        padded = jnp.concatenate([jnp.zeros((blocks, TAPS - 1, FRAME), jnp.bfloat16), volt], axis=1)
        weighted = filter_frames(padded, taps, SPECTRA)
        spectrum = jnp.einsum('nkr,isn->krsi', dft_table, weighted, precision=lax.Precision.HIGHEST)
        flagged = spectrum * flag.astype(jnp.float32).T[None, None]
        return flagged.astype(jnp.bfloat16)
    channelized = lax.map(filter_block, (volt_blocks, flag_blocks))
    channelized = jnp.transpose(channelized, (1, 2, 3, 0, 4)).reshape(CHANNELS, 2, SPECTRA, INPUTS)
    scale = 1.0 / math.sqrt(SPECTRA)

    def correlate(pair):
        data, offset = pair
        real_part = data[0]
        imag_part = data[1]
        col_side = build_columns(real_part, imag_part, (offset * blocks).astype(jnp.int32))
        row_side = jnp.concatenate([real_part, imag_part], axis=0)
        sums = products(row_side, col_side)
        return (sums * scale).astype(jnp.bfloat16)
    return lax.map(correlate, (channelized, offsets))
```

```python
import functools
import math

import jax
import jax.numpy as jnp
from jax import lax
from jax.experimental import pallas as pl
from jax.experimental.pallas import tpu as pltpu
from jax.sharding import PartitionSpec as P

MIB = 1024 * 1024


def channel_table(frame, channels, width, shift):
    period = 4 * channels
    row = lax.broadcasted_iota(jnp.int32, (2 * channels, width), 0)
    sample = lax.broadcasted_iota(jnp.int32, (2 * channels, width), 1) + shift
    phase = (2 * (row // 2) + 1) * sample % period
    angle = phase.astype(jnp.float32) * (2.0 * math.pi / period)
    norm_scale = 1.0 / math.sqrt(frame)
    return jnp.where(row % 2 == 0, jnp.cos(angle), -jnp.sin(angle)) * norm_scale


def filterbank_kernel(spec, rows, taps, chunk, block, table, tap_ref, volt, own, tail, held, weights, total, sems):
    step, steps = pl.program_id(0), pl.num_programs(0)
    frame = steps * chunk
    pairs = table.shape[0]
    cols = taps * pairs

    def fetch(index, slot):
        for f in range(spec):
            pltpu.make_async_copy(
                volt.at[:, pl.ds(pl.multiple_of(f * frame + index * chunk, chunk), chunk)],
                held.at[slot, pl.ds(f * rows, rows), :],
                sems.at[slot, f],
            ).start()

    def arrive(slot):
        for f in range(spec):
            pltpu.make_async_copy(
                volt.at[:, pl.ds(0, chunk)], held.at[slot, pl.ds(f * rows, rows), :], sems.at[slot, f]
            ).wait()

    slot = lax.rem(step, 2)

    @pl.when(step == 0)
    def _():
        fetch(0, 0)
        total[...] = jnp.zeros_like(total)

    @pl.when(step + 1 < steps)
    def _():
        fetch(step + 1, 1 - slot)

    for t in range(taps):
        exact = tap_ref[t : t + 1, :] * table[...]
        high = exact.astype(jnp.bfloat16)
        low = (exact - high.astype(jnp.float32)).astype(jnp.bfloat16)
        weights[t * pairs : (t + 1) * pairs, :] = high
        weights[cols + t * pairs : cols + (t + 1) * pairs, :] = low

    arrive(slot)

    @pl.loop(0, spec * rows // block)
    def _(m):
        span = pl.ds(pl.multiple_of(m * block, block), block)
        total[span, :] += lax.dot_general(
            held[slot, span, :], weights[...], (((1,), (1,)), ((), ())), preferred_element_type=jnp.float32
        )

    @pl.when(step == steps - 1)
    def _():
        flipped = []
        for f in range(spec):
            part = total[f * rows : (f + 1) * rows, :]
            flipped.append((part[:, :cols] + part[:, cols:]).T)
        for f in range(spec + taps - 1):
            terms = [
                flipped[f - t][t * pairs : (t + 1) * pairs, :] for t in range(taps) if 0 <= f - t < spec
            ]
            value = functools.reduce(lambda a, b: a + b, terms)
            if f < spec:
                own[:, f, :] = value
            else:
                tail[:, f - spec, :] = value


def filterbank(volt, taps, table, spec, chunk, block):
    rows, width = volt.shape
    count, frame = taps.shape
    pairs = table.shape[0]
    cols = count * pairs
    return pl.pallas_call(
        functools.partial(filterbank_kernel, spec, rows, count, chunk, block),
        grid=(frame // chunk,),
        in_specs=[
            pl.BlockSpec((pairs, chunk), lambda s: (0, 0)),
            pl.BlockSpec((count, chunk), lambda s: (0, s)),
            pl.BlockSpec(memory_space=pl.ANY),
        ],
        out_specs=[
            pl.BlockSpec((pairs, spec, rows), lambda s: (0, 0, 0)),
            pl.BlockSpec((pairs, count - 1, rows), lambda s: (0, 0, 0)),
        ],
        out_shape=[
            jax.ShapeDtypeStruct((pairs, spec, rows), jnp.float32),
            jax.ShapeDtypeStruct((pairs, count - 1, rows), jnp.float32),
        ],
        scratch_shapes=[
            pltpu.VMEM((2, spec * rows, chunk), jnp.bfloat16),
            pltpu.VMEM((2 * cols, chunk), jnp.bfloat16),
            pltpu.VMEM((spec * rows, 2 * cols), jnp.float32),
            pltpu.SemaphoreType.DMA((2, spec)),
        ],
        compiler_params=pltpu.CompilerParams(vmem_limit_bytes=56 * MIB, dimension_semantics=("arbitrary",)),
        cost_estimate=pl.CostEstimate(
            flops=4 * spec * rows * frame * cols, bytes_accessed=2 * rows * width, transcendentals=0
        ),
    )(table, taps, volt)


def correlate_kernel(scale, place, real, imag, cols, out):
    left = (((0,), (0,)), ((), ()))
    for part, side in ((0, real), (1, imag)):
        value = lax.dot_general(side[...], cols[...], left, preferred_element_type=jnp.float32)
        out[:, part, :] = (value * scale).astype(jnp.bfloat16)


def correlate(row_side, swapped, columns, rotation, scale, block):
    depth, rows = row_side.shape
    width = columns.shape[1]
    blocks = width // block
    return pl.pallas_call(
        functools.partial(correlate_kernel, scale),
        grid_spec=pltpu.PrefetchScalarGridSpec(
            num_scalar_prefetch=1,
            grid=(blocks,),
            in_specs=[
                pl.BlockSpec((depth, rows), lambda j, place: (0, 0)),
                pl.BlockSpec((depth, rows), lambda j, place: (0, 0)),
                pl.BlockSpec((depth, block), lambda j, place: (0, lax.rem(j + place[0], blocks))),
            ],
            out_specs=pl.BlockSpec((rows, 2, block), lambda j, place: (0, 0, j)),
        ),
        out_shape=jax.ShapeDtypeStruct((rows, 2, width), jnp.bfloat16),
        compiler_params=pltpu.CompilerParams(vmem_limit_bytes=56 * MIB, dimension_semantics=("arbitrary",)),
    )(rotation, row_side, swapped, columns)


def shards(voltages, taps, flags, offsets):
    chan_count = lax.axis_size("chan")
    time_count = lax.axis_size("tm")
    local_inputs = voltages.shape[0]
    spec_local = flags.shape[1]
    frame = voltages.shape[1] // spec_local
    history = taps.shape[0] - 1
    chunk = 512
    table = channel_table(frame, chan_count, chunk, jnp.minimum(offsets[0], 0))
    block = min(spec_local * local_inputs, 1024)
    own, tail = filterbank(voltages, taps, table, spec_local, chunk, block)
    earlier = lax.ppermute(tail, "tm", [(i, i + 1) for i in range(time_count - 1)])
    spectrum = own + jnp.pad(earlier, ((0, 0), (0, spec_local - history), (0, 0)))
    flagged = (spectrum * flags.astype(jnp.float32).T[None]).astype(jnp.bfloat16)
    flagged = flagged.reshape(chan_count, 2, spec_local, local_inputs)
    turned = lax.all_to_all(flagged, "chan", split_axis=0, concat_axis=0, tiled=True)
    gathered = lax.all_gather(turned, "tm")
    columns = jnp.transpose(gathered, (0, 2, 3, 1, 4)).reshape(time_count, 2, spec_local, -1)
    inputs = columns.shape[-1]
    own_rows = inputs // time_count
    row_side = lax.dynamic_slice_in_dim(columns, lax.axis_index("tm") * own_rows, own_rows, axis=3)
    swapped = jnp.stack([row_side[:, 1], -row_side[:, 0]], axis=1)
    flat = (-1, own_rows)
    scale = 1.0 / math.sqrt(spec_local * time_count)
    width = local_inputs if local_inputs % 128 == 0 else 0
    rotation = offsets * 1
    columns = columns.reshape(-1, inputs)
    if not width:
        columns = jnp.roll(columns, -offsets[0] * local_inputs, axis=1)
        rotation = offsets * 0
        width = 256
    return correlate(row_side.reshape(flat), swapped.reshape(flat), columns, rotation, scale, width)[None]


def solution(mesh):
    in_specs = (P("chan", "tm"), P(), P("chan", "tm"), P("chan"))
    out_specs = P("chan", "tm", None, None)
    return jax.shard_map(shards, mesh=mesh, in_specs=in_specs, out_specs=out_specs, check_vma=False)
```

```python
import functools
import math

import jax
import jax.numpy as jnp
from jax import lax
from jax.experimental import pallas as pl
from jax.experimental.pallas import tpu as pltpu
from jax.sharding import Mesh
from jax.sharding import PartitionSpec as P

MIB = 1024 * 1024
ACROSS = (((1,), (1,)), ((), ()))
DOWN = (((0,), (0,)), ((), ()))
RING = 3
PIECES = 4


def channel_table(frame, channels, width, shift):
    period = 4 * channels
    row = lax.broadcasted_iota(jnp.int32, (2 * channels, width), 0)
    sample = lax.broadcasted_iota(jnp.int32, (2 * channels, width), 1) + shift
    phase = (2 * (row // 2) + 1) * sample % period
    angle = phase.astype(jnp.float32) * (2.0 * math.pi / period)
    norm_scale = 1.0 / math.sqrt(frame)
    return jnp.where(row % 2 == 0, jnp.cos(angle), -jnp.sin(angle)) * norm_scale


def narrow_filterbank_kernel(spec, rows, taps, chunk, block, table, tap_ref, volt, own, tail, held, weights, total, sems):
    step, steps = pl.program_id(0), pl.num_programs(0)
    frame = steps * chunk
    pairs = table.shape[0]
    cols = taps * pairs

    def fetch(index, slot):
        for f in range(spec):
            pltpu.make_async_copy(
                volt.at[:, pl.ds(pl.multiple_of(f * frame + index * chunk, chunk), chunk)],
                held.at[slot, pl.ds(f * rows, rows), :],
                sems.at[slot, f],
            ).start()

    def arrive(slot):
        for f in range(spec):
            pltpu.make_async_copy(
                volt.at[:, pl.ds(0, chunk)], held.at[slot, pl.ds(f * rows, rows), :], sems.at[slot, f]
            ).wait()

    slot = lax.rem(step, 2)

    @pl.when(step == 0)
    def _():
        fetch(0, 0)
        total[...] = jnp.zeros_like(total)

    @pl.when(step + 1 < steps)
    def _():
        fetch(step + 1, 1 - slot)

    for t in range(taps):
        exact = tap_ref[t : t + 1, :] * table[...]
        high = exact.astype(jnp.bfloat16)
        low = (exact - high.astype(jnp.float32)).astype(jnp.bfloat16)
        weights[t * pairs : (t + 1) * pairs, :] = high
        weights[cols + t * pairs : cols + (t + 1) * pairs, :] = low

    arrive(slot)

    @pl.loop(0, spec * rows // block)
    def _(m):
        span = pl.ds(pl.multiple_of(m * block, block), block)
        total[span, :] += lax.dot_general(
            held[slot, span, :], weights[...], (((1,), (1,)), ((), ())), preferred_element_type=jnp.float32
        )

    @pl.when(step == steps - 1)
    def _():
        flipped = []
        for f in range(spec):
            part = total[f * rows : (f + 1) * rows, :]
            flipped.append((part[:, :cols] + part[:, cols:]).T)
        for f in range(spec + taps - 1):
            terms = [
                flipped[f - t][t * pairs : (t + 1) * pairs, :] for t in range(taps) if 0 <= f - t < spec
            ]
            value = functools.reduce(lambda a, b: a + b, terms)
            if f < spec:
                own[:, f, :] = value
            else:
                tail[:, f - spec, :] = value


def narrow_filterbank(volt, taps, table, spec, chunk, block):
    rows, width = volt.shape
    count, frame = taps.shape
    pairs = table.shape[0]
    cols = count * pairs
    return pl.pallas_call(
        functools.partial(narrow_filterbank_kernel, spec, rows, count, chunk, block),
        grid=(frame // chunk,),
        in_specs=[
            pl.BlockSpec((pairs, chunk), lambda s: (0, 0)),
            pl.BlockSpec((count, chunk), lambda s: (0, s)),
            pl.BlockSpec(memory_space=pl.ANY),
        ],
        out_specs=[
            pl.BlockSpec((pairs, spec, rows), lambda s: (0, 0, 0)),
            pl.BlockSpec((pairs, count - 1, rows), lambda s: (0, 0, 0)),
        ],
        out_shape=[
            jax.ShapeDtypeStruct((pairs, spec, rows), jnp.float32),
            jax.ShapeDtypeStruct((pairs, count - 1, rows), jnp.float32),
        ],
        scratch_shapes=[
            pltpu.VMEM((2, spec * rows, chunk), jnp.bfloat16),
            pltpu.VMEM((2 * cols, chunk), jnp.bfloat16),
            pltpu.VMEM((spec * rows, 2 * cols), jnp.float32),
            pltpu.SemaphoreType.DMA((2, spec)),
        ],
        compiler_params=pltpu.CompilerParams(vmem_limit_bytes=56 * MIB, dimension_semantics=("arbitrary",)),
        cost_estimate=pl.CostEstimate(
            flops=4 * spec * rows * frame * cols, bytes_accessed=2 * rows * width, transcendentals=0
        ),
    )(table, taps, volt)


def filterbank_kernel(spec, rows, offset, tap_hbm, volt, own, tail, tap_ref, held, weights, folded, sems, tap_sem):
    taps, frame = tap_ref.shape
    pairs = own.shape[0]
    cols = taps * pairs
    width = frame // PIECES
    pair_steps = (spec - 2) // 2

    def piece(step, part, count, first):
        slot = lax.rem(jnp.int32(step), RING)
        copies = []
        for n in range(count):
            start = pl.multiple_of((first + n) * frame + part * width, width)
            copies.append(
                pltpu.make_async_copy(
                    volt.at[:, pl.ds(start, width)],
                    held.at[slot, pl.ds(n * rows, rows), pl.ds(part * width, width)],
                    sems.at[slot, part],
                )
            )
        return copies

    def fetch_single(step, first):
        for part in range(PIECES):
            piece(step, part, 1, first)[0].start()

    def fetch_pair(step):
        slot = lax.rem(jnp.int32(step), RING)
        for n in range(2):
            start = pl.multiple_of((2 * step - 1 + n) * frame, frame)
            pltpu.make_async_copy(
                volt.at[:, pl.ds(start, frame)], held.at[slot, pl.ds(n * rows, rows), :], sems.at[slot, 0]
            ).start()

    def add(value, first, count):
        value = value[:cols] + value[cols:]
        for t in range(taps):
            span = pl.ds(pl.multiple_of((first + t) * rows, rows), count * rows)
            folded[:, span] += value[t * pairs : (t + 1) * pairs, :]

    def single(step, first, prepare):
        total = None
        slot = step % RING
        for part in range(PIECES):
            prepare(part)
            piece(step, part, 1, first)[0].wait()
            span = slice(part * width, (part + 1) * width)
            value = lax.dot_general(
                weights[:, span], held[slot, :rows, span], ACROSS, preferred_element_type=jnp.float32
            )
            total = value if total is None else total + value
        add(total, first, 1)

    taps_copy = pltpu.make_async_copy(tap_hbm, tap_ref, tap_sem)
    taps_copy.start()
    fetch_single(0, 0)
    fetch_pair(1)
    folded[...] = jnp.zeros_like(folded)
    table = channel_table(frame, pairs // 2, 128, jnp.minimum(offset[0], 0))
    table = jnp.concatenate([table] * (width // 128), axis=1)
    taps_copy.wait()

    def build(part):
        span = slice(part * width, (part + 1) * width)
        for t in range(taps):
            exact = tap_ref[t : t + 1, span] * table
            high = exact.astype(jnp.bfloat16)
            low = (exact - high.astype(jnp.float32)).astype(jnp.bfloat16)
            weights[t * pairs : (t + 1) * pairs, span] = high
            weights[cols + t * pairs : cols + (t + 1) * pairs, span] = low

    fetch_pair(2)
    single(0, 0, build)

    @pl.loop(1, pair_steps + 1)
    def _(step):
        @pl.when(step + 2 <= pair_steps)
        def _():
            fetch_pair(step + 2)

        @pl.when(step + 2 == pair_steps + 1)
        def _():
            fetch_single(pair_steps + 1, spec - 1)

        slot = lax.rem(step, RING)
        block = held.at[slot]
        pltpu.make_async_copy(block, block, sems.at[slot, 0]).wait()
        value = lax.dot_general(weights[...], block[...], ACROSS, preferred_element_type=jnp.float32)
        add(value, 2 * step - 1, 2)

    single(pair_steps + 1, spec - 1, lambda part: None)
    for f in range(spec + taps - 1):
        value = folded[:, f * rows : (f + 1) * rows]
        if f < spec:
            own[:, f, :] = value
        else:
            tail[:, f - spec, :] = value


def filterbank(volt, taps, offsets, channels, spec):
    rows, width = volt.shape
    count, frame = taps.shape
    pairs = 2 * channels
    cols = count * pairs
    return pl.pallas_call(
        functools.partial(filterbank_kernel, spec, rows),
        in_specs=[
            pl.BlockSpec(memory_space=pltpu.SMEM),
            pl.BlockSpec(memory_space=pl.ANY),
            pl.BlockSpec(memory_space=pl.ANY),
        ],
        out_shape=[
            jax.ShapeDtypeStruct((pairs, spec, rows), jnp.float32),
            jax.ShapeDtypeStruct((pairs, count - 1, rows), jnp.float32),
        ],
        scratch_shapes=[
            pltpu.VMEM((count, frame), jnp.float32),
            pltpu.VMEM((RING, 2 * rows, frame), jnp.bfloat16),
            pltpu.VMEM((2 * cols, frame), jnp.bfloat16),
            pltpu.VMEM((pairs, (spec + count - 1) * rows), jnp.float32),
            pltpu.SemaphoreType.DMA((RING, PIECES)),
            pltpu.SemaphoreType.DMA,
        ],
        compiler_params=pltpu.CompilerParams(vmem_limit_bytes=56 * MIB),
        cost_estimate=pl.CostEstimate(
            flops=4 * spec * rows * frame * cols, bytes_accessed=2 * rows * width, transcendentals=0
        ),
    )(offsets, taps, volt)


def correlate_kernel(scale, place, mine_rows, other_rows, mine_cols, other_cols, out, side):
    blocks, wide, _, spec, lanes = mine_cols.shape
    depth = 2 * wide * 2 * spec

    @pl.when(pl.program_id(0) == 0)
    def _():
        for j in range(blocks):
            turned = lax.rem(j + place[0], blocks)
            at = 0
            for source in (mine_cols, other_cols):
                for x in range(wide):
                    for part in range(2):
                        side[at : at + spec, j * lanes : (j + 1) * lanes] = source[turned, x, part]
                        at += spec

    real, imag = [], []
    for source in (mine_rows, other_rows):
        for x in range(wide):
            first, second = source[0, x, 0], source[0, x, 1]
            real += [first, second]
            imag += [second, -first]
    for part, rows in ((0, real), (1, imag)):
        value = lax.dot_general(
            jnp.concatenate(rows, axis=0), side[...], DOWN, preferred_element_type=jnp.float32
        )
        out[:, part, :] = (value * scale).astype(jnp.bfloat16)


def correlate(mine_rows, other_rows, mine_cols, other_cols, rotation, place, scale, own_rows):
    blocks, wide, parts, spec, lanes = mine_cols.shape
    own_blocks = own_rows // lanes
    row_spec = pl.BlockSpec((1, wide, parts, spec, lanes), lambda i, place: (place[1] * own_blocks + i, 0, 0, 0, 0))
    col_spec = pl.BlockSpec((blocks, wide, parts, spec, lanes), lambda i, place: (0, 0, 0, 0, 0))
    return pl.pallas_call(
        functools.partial(correlate_kernel, scale),
        grid_spec=pltpu.PrefetchScalarGridSpec(
            num_scalar_prefetch=1,
            grid=(own_blocks,),
            in_specs=[row_spec, row_spec, col_spec, col_spec],
            out_specs=pl.BlockSpec((lanes, 2, blocks * lanes), lambda i, place: (i, 0, 0)),
            scratch_shapes=[pltpu.VMEM((2 * wide * 2 * spec, blocks * lanes), jnp.bfloat16)],
        ),
        out_shape=jax.ShapeDtypeStruct((own_rows, 2, blocks * lanes), jnp.bfloat16),
        compiler_params=pltpu.CompilerParams(vmem_limit_bytes=56 * MIB, dimension_semantics=("arbitrary",)),
    )(jnp.stack([rotation, place]), mine_rows, other_rows, mine_cols, other_cols)


def regroup(pieces, lanes):
    blocks, wide, parts, spec, narrow = pieces.shape
    join = lanes // narrow
    pieces = pieces.reshape(blocks // join, join, wide, parts, spec, narrow)
    return jnp.transpose(pieces, (0, 2, 3, 4, 1, 5)).reshape(blocks // join, wide, parts, spec, lanes)


def shards(voltages, taps, flags, offsets):
    chan_count, wide, cores = (lax.axis_size(name) for name in ("chan", "wide", "core"))
    time_count = wide * cores
    local_inputs = voltages.shape[0]
    inputs = local_inputs * chan_count
    spec_local = flags.shape[1]
    frame = voltages.shape[1] // spec_local
    history = taps.shape[0] - 1
    aligned = local_inputs % 128 == 0 and 128 % (4 * chan_count) == 0
    if aligned:
        own, tail = filterbank(voltages, taps, offsets, chan_count, spec_local)
    else:
        table = channel_table(frame, chan_count, 512, jnp.minimum(offsets[0], 0))
        own, tail = narrow_filterbank(voltages, taps, table, spec_local, 512, spec_local * local_inputs)
    earlier = lax.ppermute(tail, ("wide", "core"), [(i, i + 1) for i in range(time_count - 1)])
    spectrum = own + jnp.pad(earlier, ((0, 0), (0, spec_local - history), (0, 0)))
    flagged = (spectrum * flags.astype(jnp.float32).T[None]).astype(jnp.bfloat16)
    flagged = flagged.reshape(chan_count, 1, 2, spec_local, local_inputs)
    sent = jnp.broadcast_to(flagged, (chan_count, wide, 2, spec_local, local_inputs))
    sent = sent.reshape(chan_count * wide, 2, spec_local, local_inputs)
    mine = lax.all_to_all(sent, ("chan", "wide"), split_axis=0, concat_axis=0, tiled=True)
    other = lax.ppermute(mine, "core", [(0, 1), (1, 0)])
    shape = (chan_count, wide, 2, spec_local, local_inputs)
    mine, other = mine.reshape(shape), other.reshape(shape)
    scale = 1.0 / math.sqrt(spec_local * time_count)
    own_rows = inputs // time_count
    place = lax.axis_index(("wide", "core"))
    if aligned:
        return correlate(mine, other, mine, other, offsets[0], place, scale, own_rows)[None]
    lanes = 256
    rows = [regroup(pieces, lanes) for pieces in (mine, other)]
    cols = [regroup(jnp.roll(pieces, -offsets[0], axis=0), lanes) for pieces in (mine, other)]
    return correlate(*rows, *cols, offsets[0] * 0, place, scale, own_rows)[None]


def solution(mesh):
    devices = mesh.devices.reshape(mesh.shape["chan"], -1, 2)
    split = Mesh(devices, ("chan", "wide", "core"))
    time = ("wide", "core")
    in_specs = (P("chan", time), P(), P("chan", time), P("chan"))
    out_specs = P("chan", time, None, None)
    return jax.shard_map(shards, mesh=split, in_specs=in_specs, out_specs=out_specs, check_vma=False)
```

```python
import functools
import math

import jax
import jax.numpy as jnp
from jax import lax
from jax.experimental import pallas as pl
from jax.experimental.pallas import tpu as pltpu
from jax.sharding import Mesh
from jax.sharding import PartitionSpec as P

MIB = 1024 * 1024
ACROSS = (((1,), (1,)), ((), ()))
DOWN = (((0,), (0,)), ((), ()))
GROUP = 1
AHEAD = 3


def channel_table(frame, channels, width, shift):
    period = 4 * channels
    row = lax.broadcasted_iota(jnp.int32, (2 * channels, width), 0)
    sample = lax.broadcasted_iota(jnp.int32, (2 * channels, width), 1) + shift
    phase = (2 * (row // 2) + 1) * sample % period
    angle = phase.astype(jnp.float32) * (2.0 * math.pi / period)
    norm_scale = 1.0 / math.sqrt(frame)
    return jnp.where(row % 2 == 0, jnp.cos(angle), -jnp.sin(angle)) * norm_scale


def narrow_filterbank_kernel(spec, rows, taps, chunk, block, table, tap_ref, volt, own, tail, held, weights, total, sems):
    step, steps = pl.program_id(0), pl.num_programs(0)
    frame = steps * chunk
    pairs = table.shape[0]
    cols = taps * pairs

    def fetch(index, slot):
        for f in range(spec):
            pltpu.make_async_copy(
                volt.at[:, pl.ds(pl.multiple_of(f * frame + index * chunk, chunk), chunk)],
                held.at[slot, pl.ds(f * rows, rows), :],
                sems.at[slot, f],
            ).start()

    def arrive(slot):
        for f in range(spec):
            pltpu.make_async_copy(
                volt.at[:, pl.ds(0, chunk)], held.at[slot, pl.ds(f * rows, rows), :], sems.at[slot, f]
            ).wait()

    slot = lax.rem(step, 2)

    @pl.when(step == 0)
    def _():
        fetch(0, 0)
        total[...] = jnp.zeros_like(total)

    @pl.when(step + 1 < steps)
    def _():
        fetch(step + 1, 1 - slot)

    for t in range(taps):
        exact = tap_ref[t : t + 1, :] * table[...]
        high = exact.astype(jnp.bfloat16)
        low = (exact - high.astype(jnp.float32)).astype(jnp.bfloat16)
        weights[t * pairs : (t + 1) * pairs, :] = high
        weights[cols + t * pairs : cols + (t + 1) * pairs, :] = low

    arrive(slot)

    @pl.loop(0, spec * rows // block)
    def _(m):
        span = pl.ds(pl.multiple_of(m * block, block), block)
        total[span, :] += lax.dot_general(
            held[slot, span, :], weights[...], (((1,), (1,)), ((), ())), preferred_element_type=jnp.float32
        )

    @pl.when(step == steps - 1)
    def _():
        flipped = []
        for f in range(spec):
            part = total[f * rows : (f + 1) * rows, :]
            flipped.append((part[:, :cols] + part[:, cols:]).T)
        for f in range(spec + taps - 1):
            terms = [
                flipped[f - t][t * pairs : (t + 1) * pairs, :] for t in range(taps) if 0 <= f - t < spec
            ]
            value = functools.reduce(lambda a, b: a + b, terms)
            if f < spec:
                own[:, f, :] = value
            else:
                tail[:, f - spec, :] = value


def narrow_filterbank(volt, taps, table, spec, chunk, block):
    rows, width = volt.shape
    count, frame = taps.shape
    pairs = table.shape[0]
    cols = count * pairs
    return pl.pallas_call(
        functools.partial(narrow_filterbank_kernel, spec, rows, count, chunk, block),
        grid=(frame // chunk,),
        in_specs=[
            pl.BlockSpec((pairs, chunk), lambda s: (0, 0)),
            pl.BlockSpec((count, chunk), lambda s: (0, s)),
            pl.BlockSpec(memory_space=pl.ANY),
        ],
        out_specs=[
            pl.BlockSpec((pairs, spec, rows), lambda s: (0, 0, 0)),
            pl.BlockSpec((pairs, count - 1, rows), lambda s: (0, 0, 0)),
        ],
        out_shape=[
            jax.ShapeDtypeStruct((pairs, spec, rows), jnp.float32),
            jax.ShapeDtypeStruct((pairs, count - 1, rows), jnp.float32),
        ],
        scratch_shapes=[
            pltpu.VMEM((2, spec * rows, chunk), jnp.bfloat16),
            pltpu.VMEM((2 * cols, chunk), jnp.bfloat16),
            pltpu.VMEM((spec * rows, 2 * cols), jnp.float32),
            pltpu.SemaphoreType.DMA((2, spec)),
        ],
        compiler_params=pltpu.CompilerParams(vmem_limit_bytes=56 * MIB, dimension_semantics=("arbitrary",)),
        cost_estimate=pl.CostEstimate(
            flops=4 * spec * rows * frame * cols, bytes_accessed=2 * rows * width, transcendentals=0
        ),
    )(table, taps, volt)


def filterbank_kernel(spec, rows, offset, tap_hbm, volt, own, tail, tap_ref, held, weights, folded, sems, tap_sem):
    taps, frame = tap_ref.shape
    pairs = own.shape[0]
    cols = taps * pairs
    ring = held.shape[0]
    steps = spec // GROUP
    strip = 512

    def copies(step):
        slot = lax.rem(step, ring)
        made = []
        for n in range(GROUP):
            start = pl.multiple_of((step * GROUP + n) * frame, frame)
            made.append(
                pltpu.make_async_copy(
                    volt.at[:, pl.ds(start, frame)], held.at[slot, pl.ds(n * rows, rows), :], sems.at[slot]
                )
            )
        return made

    taps_copy = pltpu.make_async_copy(tap_hbm, tap_ref, tap_sem)
    taps_copy.start()

    @pl.loop(0, AHEAD)
    def _(step):
        for copy in copies(step):
            copy.start()

    folded[...] = jnp.zeros_like(folded)
    table = channel_table(frame, pairs // 2, 128, jnp.minimum(offset[0], 0))
    table = jnp.concatenate([table] * (strip // 128), axis=1)
    taps_copy.wait()

    @pl.loop(0, frame // strip)
    def _(s):
        span = pl.ds(pl.multiple_of(s * strip, strip), strip)
        for t in range(taps):
            exact = tap_ref[t : t + 1, span] * table
            high = exact.astype(jnp.bfloat16)
            low = (exact - high.astype(jnp.float32)).astype(jnp.bfloat16)
            weights[t * pairs : (t + 1) * pairs, span] = high
            weights[cols + t * pairs : cols + (t + 1) * pairs, span] = low

    @pl.loop(0, steps)
    def _(step):
        slot = lax.rem(step, ring)
        block = held.at[slot]
        pltpu.make_async_copy(block, block, sems.at[slot]).wait()

        @pl.when(step + AHEAD < steps)
        def _():
            for copy in copies(step + AHEAD):
                copy.start()

        value = lax.dot_general(weights[...], block[...], ACROSS, preferred_element_type=jnp.float32)
        value = value[:cols] + value[cols:]
        for t in range(taps):
            span = pl.ds(pl.multiple_of((step * GROUP + t) * rows, rows), GROUP * rows)
            folded[:, span] += value[t * pairs : (t + 1) * pairs, :]

    for f in range(spec + taps - 1):
        value = folded[:, f * rows : (f + 1) * rows]
        if f < spec:
            own[:, f, :] = value
        else:
            tail[:, f - spec, :] = value


def filterbank(volt, taps, offsets, channels, spec):
    rows, width = volt.shape
    count, frame = taps.shape
    pairs = 2 * channels
    cols = count * pairs
    return pl.pallas_call(
        functools.partial(filterbank_kernel, spec, rows),
        in_specs=[
            pl.BlockSpec(memory_space=pltpu.SMEM),
            pl.BlockSpec(memory_space=pl.ANY),
            pl.BlockSpec(memory_space=pl.ANY),
        ],
        out_shape=[
            jax.ShapeDtypeStruct((pairs, spec, rows), jnp.float32),
            jax.ShapeDtypeStruct((pairs, count - 1, rows), jnp.float32),
        ],
        scratch_shapes=[
            pltpu.VMEM((count, frame), jnp.float32),
            pltpu.VMEM((AHEAD + 1, GROUP * rows, frame), jnp.bfloat16),
            pltpu.VMEM((2 * cols, frame), jnp.bfloat16),
            pltpu.VMEM((pairs, (spec + count - 1) * rows), jnp.float32),
            pltpu.SemaphoreType.DMA((AHEAD + 1,)),
            pltpu.SemaphoreType.DMA,
        ],
        compiler_params=pltpu.CompilerParams(vmem_limit_bytes=56 * MIB),
        cost_estimate=pl.CostEstimate(
            flops=4 * spec * rows * frame * cols, bytes_accessed=2 * rows * width, transcendentals=0
        ),
    )(offsets, taps, volt)


def correlate_kernel(scale, rotation, *refs):
    sources, (out, side, weave) = refs[:-3], refs[-3:]
    rows, columns = sources[:2], sources[-2:]
    blocks, wide, _, spec, lanes = columns[0].shape
    step = pl.program_id(0)

    @pl.when(step == 0)
    def _():
        for j in range(blocks):
            turned = lax.rem(j + rotation[0], blocks)
            at = 0
            for source in columns:
                for x in range(wide):
                    for part in range(2):
                        side[at : at + spec, j * lanes : (j + 1) * lanes] = source[turned, x, part]
                        at += spec
        taken = lax.broadcasted_iota(jnp.int32, weave.shape, 0)
        made = lax.broadcasted_iota(jnp.int32, weave.shape, 1)
        weave[...] = (taken == made // 2 + made % 2 * lanes).astype(jnp.float32).astype(jnp.bfloat16)

    place = (lax.axis_index("wide") * 2 + lax.axis_index("core")) * pl.num_programs(0) + step
    real, imag = [], []
    for source in rows:
        for x in range(wide):
            first, second = source[place, x, 0], source[place, x, 1]
            real += [first, second]
            imag += [second, -first]
    both = jnp.concatenate([jnp.concatenate(real, axis=0), jnp.concatenate(imag, axis=0)], axis=1)
    woven = jnp.dot(both, weave[...], preferred_element_type=jnp.float32)
    exact = math.frexp(scale)[0] == 0.5
    if exact:
        woven *= scale
    value = lax.dot_general(woven.astype(jnp.bfloat16), side[...], DOWN, preferred_element_type=jnp.float32)
    if not exact:
        value *= scale
    out[...] = value.astype(jnp.bfloat16).reshape(out.shape)


def correlate(sources, rotation, scale, own_rows):
    blocks, wide, parts, spec, lanes = sources[0].shape
    whole = pl.BlockSpec((blocks, wide, parts, spec, lanes), lambda i, rotation: (0, 0, 0, 0, 0))
    return pl.pallas_call(
        functools.partial(correlate_kernel, scale),
        grid_spec=pltpu.PrefetchScalarGridSpec(
            num_scalar_prefetch=1,
            grid=(own_rows // lanes,),
            in_specs=[whole] * len(sources),
            out_specs=pl.BlockSpec((lanes, 2, blocks * lanes), lambda i, rotation: (i, 0, 0)),
            scratch_shapes=[
                pltpu.VMEM((2 * wide * 2 * spec, blocks * lanes), jnp.bfloat16),
                pltpu.VMEM((2 * lanes, 2 * lanes), jnp.bfloat16),
            ],
        ),
        out_shape=jax.ShapeDtypeStruct((own_rows, 2, blocks * lanes), jnp.bfloat16),
        compiler_params=pltpu.CompilerParams(vmem_limit_bytes=56 * MIB, dimension_semantics=("arbitrary",)),
    )(rotation, *sources)


def regroup(pieces, lanes):
    blocks, wide, parts, spec, narrow = pieces.shape
    join = lanes // narrow
    pieces = pieces.reshape(blocks // join, join, wide, parts, spec, narrow)
    return jnp.transpose(pieces, (0, 2, 3, 4, 1, 5)).reshape(blocks // join, wide, parts, spec, lanes)


def shards(voltages, taps, flags, offsets):
    chan_count, wide, cores = (lax.axis_size(name) for name in ("chan", "wide", "core"))
    time_count = wide * cores
    local_inputs = voltages.shape[0]
    inputs = local_inputs * chan_count
    spec_local = flags.shape[1]
    frame = voltages.shape[1] // spec_local
    history = taps.shape[0] - 1
    aligned = local_inputs % 128 == 0 and 128 % (4 * chan_count) == 0
    if aligned:
        own, tail = filterbank(voltages, taps, offsets, chan_count, spec_local)
    else:
        table = channel_table(frame, chan_count, 512, jnp.minimum(offsets[0], 0))
        own, tail = narrow_filterbank(voltages, taps, table, spec_local, 512, spec_local * local_inputs)
    earlier = lax.ppermute(tail, ("wide", "core"), [(i, i + 1) for i in range(time_count - 1)])
    spectrum = own + jnp.pad(earlier, ((0, 0), (0, spec_local - history), (0, 0)))
    flagged = (spectrum * flags.astype(jnp.float32).T[None]).astype(jnp.bfloat16)
    flagged = flagged.reshape(chan_count, 1, 2, spec_local, local_inputs)
    sent = jnp.broadcast_to(flagged, (chan_count, wide, 2, spec_local, local_inputs))
    sent = sent.reshape(chan_count * wide, 2, spec_local, local_inputs)
    mine = lax.all_to_all(sent, ("chan", "wide"), split_axis=0, concat_axis=0, tiled=True)
    other = lax.ppermute(mine, "core", [(0, 1), (1, 0)])
    shape = (chan_count, wide, 2, spec_local, local_inputs)
    mine, other = mine.reshape(shape), other.reshape(shape)
    scale = 1.0 / math.sqrt(spec_local * time_count)
    own_rows = inputs // time_count
    if aligned:
        return correlate((mine, other), offsets, scale, own_rows)[None]
    lanes = 256
    rows = [regroup(pieces, lanes) for pieces in (mine, other)]
    cols = [regroup(jnp.roll(pieces, -offsets[0], axis=0), lanes) for pieces in (mine, other)]
    return correlate((*rows, *cols), offsets * 0, scale, own_rows)[None]


def solution(mesh):
    devices = mesh.devices.reshape(mesh.shape["chan"], -1, 2)
    split = Mesh(devices, ("chan", "wide", "core"))
    time = ("wide", "core")
    in_specs = (P("chan", time), P(), P("chan", time), P("chan"))
    out_specs = P("chan", time, None, None)
    return jax.shard_map(shards, mesh=split, in_specs=in_specs, out_specs=out_specs, check_vma=False)
```

```python
import functools
import math

import jax
import jax.numpy as jnp
from jax import lax
from jax.experimental import pallas as pl
from jax.experimental.pallas import tpu as pltpu
from jax.sharding import Mesh
from jax.sharding import PartitionSpec as P

MIB = 1024 * 1024
ACROSS = (((1,), (1,)), ((), ()))
DOWN = (((0,), (0,)), ((), ()))
GROUP = 1
AHEAD = 3


def channel_table(frame, channels, width, shift):
    period = 4 * channels
    row = lax.broadcasted_iota(jnp.int32, (2 * channels, width), 0)
    sample = lax.broadcasted_iota(jnp.int32, (2 * channels, width), 1) + shift
    phase = (2 * (row // 2) + 1) * sample % period
    angle = phase.astype(jnp.float32) * (2.0 * math.pi / period)
    norm_scale = 1.0 / math.sqrt(frame)
    return jnp.where(row % 2 == 0, jnp.cos(angle), -jnp.sin(angle)) * norm_scale


def narrow_filterbank_kernel(spec, rows, taps, chunk, block, table, tap_ref, volt, own, tail, held, weights, total, sems):
    step, steps = pl.program_id(0), pl.num_programs(0)
    frame = steps * chunk
    pairs = table.shape[0]
    cols = taps * pairs

    def fetch(index, slot):
        for f in range(spec):
            pltpu.make_async_copy(
                volt.at[:, pl.ds(pl.multiple_of(f * frame + index * chunk, chunk), chunk)],
                held.at[slot, pl.ds(f * rows, rows), :],
                sems.at[slot, f],
            ).start()

    def arrive(slot):
        for f in range(spec):
            pltpu.make_async_copy(
                volt.at[:, pl.ds(0, chunk)], held.at[slot, pl.ds(f * rows, rows), :], sems.at[slot, f]
            ).wait()

    slot = lax.rem(step, 2)

    @pl.when(step == 0)
    def _():
        fetch(0, 0)
        total[...] = jnp.zeros_like(total)

    @pl.when(step + 1 < steps)
    def _():
        fetch(step + 1, 1 - slot)

    for t in range(taps):
        exact = tap_ref[t : t + 1, :] * table[...]
        high = exact.astype(jnp.bfloat16)
        low = (exact - high.astype(jnp.float32)).astype(jnp.bfloat16)
        weights[t * pairs : (t + 1) * pairs, :] = high
        weights[cols + t * pairs : cols + (t + 1) * pairs, :] = low

    arrive(slot)

    @pl.loop(0, spec * rows // block)
    def _(m):
        span = pl.ds(pl.multiple_of(m * block, block), block)
        total[span, :] += lax.dot_general(
            held[slot, span, :], weights[...], (((1,), (1,)), ((), ())), preferred_element_type=jnp.float32
        )

    @pl.when(step == steps - 1)
    def _():
        flipped = []
        for f in range(spec):
            part = total[f * rows : (f + 1) * rows, :]
            flipped.append((part[:, :cols] + part[:, cols:]).T)
        for f in range(spec + taps - 1):
            terms = [
                flipped[f - t][t * pairs : (t + 1) * pairs, :] for t in range(taps) if 0 <= f - t < spec
            ]
            value = functools.reduce(lambda a, b: a + b, terms)
            if f < spec:
                own[:, f, :] = value
            else:
                tail[:, f - spec, :] = value


def narrow_filterbank(volt, taps, table, spec, chunk, block):
    rows, width = volt.shape
    count, frame = taps.shape
    pairs = table.shape[0]
    cols = count * pairs
    return pl.pallas_call(
        functools.partial(narrow_filterbank_kernel, spec, rows, count, chunk, block),
        grid=(frame // chunk,),
        in_specs=[
            pl.BlockSpec((pairs, chunk), lambda s: (0, 0)),
            pl.BlockSpec((count, chunk), lambda s: (0, s)),
            pl.BlockSpec(memory_space=pl.ANY),
        ],
        out_specs=[
            pl.BlockSpec((pairs, spec, rows), lambda s: (0, 0, 0)),
            pl.BlockSpec((pairs, count - 1, rows), lambda s: (0, 0, 0)),
        ],
        out_shape=[
            jax.ShapeDtypeStruct((pairs, spec, rows), jnp.float32),
            jax.ShapeDtypeStruct((pairs, count - 1, rows), jnp.float32),
        ],
        scratch_shapes=[
            pltpu.VMEM((2, spec * rows, chunk), jnp.bfloat16),
            pltpu.VMEM((2 * cols, chunk), jnp.bfloat16),
            pltpu.VMEM((spec * rows, 2 * cols), jnp.float32),
            pltpu.SemaphoreType.DMA((2, spec)),
        ],
        compiler_params=pltpu.CompilerParams(vmem_limit_bytes=56 * MIB, dimension_semantics=("arbitrary",)),
        cost_estimate=pl.CostEstimate(
            flops=4 * spec * rows * frame * cols, bytes_accessed=2 * rows * width, transcendentals=0
        ),
    )(table, taps, volt)


def filterbank_kernel(spec, rows, offset, tap_hbm, volt, own, tail, tap_ref, held, weights, folded, sems, tap_sem):
    taps, frame = tap_ref.shape
    pairs = own.shape[0]
    cols = taps * pairs
    ring = held.shape[0]
    steps = spec // GROUP
    strip = 512

    def copies(step):
        slot = lax.rem(step, ring)
        made = []
        for n in range(GROUP):
            start = pl.multiple_of((step * GROUP + n) * frame, frame)
            made.append(
                pltpu.make_async_copy(
                    volt.at[:, pl.ds(start, frame)], held.at[slot, pl.ds(n * rows, rows), :], sems.at[slot]
                )
            )
        return made

    taps_copy = pltpu.make_async_copy(tap_hbm, tap_ref, tap_sem)
    taps_copy.start()

    @pl.loop(0, AHEAD)
    def _(step):
        for copy in copies(step):
            copy.start()

    folded[...] = jnp.zeros_like(folded)
    table = channel_table(frame, pairs // 2, 128, jnp.minimum(offset[0], 0))
    table = jnp.concatenate([table] * (strip // 128), axis=1)
    taps_copy.wait()

    @pl.loop(0, frame // strip)
    def _(s):
        span = pl.ds(pl.multiple_of(s * strip, strip), strip)
        for t in range(taps):
            exact = tap_ref[t : t + 1, span] * table
            high = exact.astype(jnp.bfloat16)
            low = (exact - high.astype(jnp.float32)).astype(jnp.bfloat16)
            weights[t * pairs : (t + 1) * pairs, span] = high
            weights[cols + t * pairs : cols + (t + 1) * pairs, span] = low

    @pl.loop(0, steps)
    def _(step):
        slot = lax.rem(step, ring)
        block = held.at[slot]
        pltpu.make_async_copy(block, block, sems.at[slot]).wait()

        @pl.when(step + AHEAD < steps)
        def _():
            for copy in copies(step + AHEAD):
                copy.start()

        value = lax.dot_general(weights[...], block[...], ACROSS, preferred_element_type=jnp.float32)
        value = value[:cols] + value[cols:]
        for t in range(taps):
            span = pl.ds(pl.multiple_of((step * GROUP + t) * rows, rows), GROUP * rows)
            folded[:, span] += value[t * pairs : (t + 1) * pairs, :]

    for f in range(spec + taps - 1):
        value = folded[:, f * rows : (f + 1) * rows]
        if f < spec:
            own[:, f, :] = value
        else:
            tail[:, f - spec, :] = value


def filterbank(volt, taps, offsets, channels, spec):
    rows, width = volt.shape
    count, frame = taps.shape
    pairs = 2 * channels
    cols = count * pairs
    return pl.pallas_call(
        functools.partial(filterbank_kernel, spec, rows),
        in_specs=[
            pl.BlockSpec(memory_space=pltpu.SMEM),
            pl.BlockSpec(memory_space=pltpu.HBM),
            pl.BlockSpec(memory_space=pltpu.HBM),
        ],
        out_specs=[pl.BlockSpec(memory_space=pltpu.VMEM)] * 2,
        out_shape=[
            jax.ShapeDtypeStruct((pairs, spec, rows), jnp.float32),
            jax.ShapeDtypeStruct((pairs, count - 1, rows), jnp.float32),
        ],
        scratch_shapes=[
            pltpu.VMEM((count, frame), jnp.float32),
            pltpu.VMEM((AHEAD + 1, GROUP * rows, frame), jnp.bfloat16),
            pltpu.VMEM((2 * cols, frame), jnp.bfloat16),
            pltpu.VMEM((pairs, (spec + count - 1) * rows), jnp.float32),
            pltpu.SemaphoreType.DMA((AHEAD + 1,)),
            pltpu.SemaphoreType.DMA,
        ],
        compiler_params=pltpu.CompilerParams(vmem_limit_bytes=36 * MIB),
        cost_estimate=pl.CostEstimate(
            flops=4 * spec * rows * frame * cols, bytes_accessed=2 * rows * width, transcendentals=0
        ),
    )(offsets, taps, volt)


def correlate_kernel(scale, rotation, *refs):
    sources, (out, side, weave) = refs[:-3], refs[-3:]
    rows, columns = sources[:2], sources[-2:]
    blocks, wide, _, spec, lanes = columns[0].shape
    step = pl.program_id(0)

    @pl.when(step == 0)
    def _():
        for j in range(blocks):
            turned = lax.rem(j + rotation[0], blocks)
            at = 0
            for source in columns:
                for x in range(wide):
                    for part in range(2):
                        side[at : at + spec, j * lanes : (j + 1) * lanes] = source[turned, x, part]
                        at += spec
        taken = lax.broadcasted_iota(jnp.int32, weave.shape, 0)
        made = lax.broadcasted_iota(jnp.int32, weave.shape, 1)
        weave[...] = (taken == made // 2 + made % 2 * lanes).astype(jnp.float32).astype(jnp.bfloat16)

    place = (lax.axis_index("wide") * 2 + lax.axis_index("core")) * pl.num_programs(0) + step
    real, imag = [], []
    for source in rows:
        for x in range(wide):
            first, second = source[place, x, 0], source[place, x, 1]
            real += [first, second]
            imag += [second, -first]
    both = jnp.concatenate([jnp.concatenate(real, axis=0), jnp.concatenate(imag, axis=0)], axis=1)
    woven = jnp.dot(both, weave[...], preferred_element_type=jnp.float32)
    exact = math.frexp(scale)[0] == 0.5
    if exact:
        woven *= scale
    value = lax.dot_general(woven.astype(jnp.bfloat16), side[...], DOWN, preferred_element_type=jnp.float32)
    if not exact:
        value *= scale
    out[...] = value.astype(jnp.bfloat16).reshape(out.shape)


def correlate(sources, rotation, scale, own_rows):
    blocks, wide, parts, spec, lanes = sources[0].shape
    whole = pl.BlockSpec(memory_space=pltpu.VMEM)
    return pl.pallas_call(
        functools.partial(correlate_kernel, scale),
        grid_spec=pltpu.PrefetchScalarGridSpec(
            num_scalar_prefetch=1,
            grid=(own_rows // lanes,),
            in_specs=[whole] * len(sources),
            out_specs=pl.BlockSpec((lanes, 2, blocks * lanes), lambda i, rotation: (i, 0, 0)),
            scratch_shapes=[
                pltpu.VMEM((2 * wide * 2 * spec, blocks * lanes), jnp.bfloat16),
                pltpu.VMEM((2 * lanes, 2 * lanes), jnp.bfloat16),
            ],
        ),
        out_shape=jax.ShapeDtypeStruct((own_rows, 2, blocks * lanes), jnp.bfloat16),
        compiler_params=pltpu.CompilerParams(vmem_limit_bytes=24 * MIB, dimension_semantics=("arbitrary",)),
    )(rotation, *sources)


def regroup(pieces, lanes):
    blocks, wide, parts, spec, narrow = pieces.shape
    join = lanes // narrow
    pieces = pieces.reshape(blocks // join, join, wide, parts, spec, narrow)
    return jnp.transpose(pieces, (0, 2, 3, 4, 1, 5)).reshape(blocks // join, wide, parts, spec, lanes)


def shards(voltages, taps, flags, offsets):
    chan_count, wide, cores = (lax.axis_size(name) for name in ("chan", "wide", "core"))
    time_count = wide * cores
    local_inputs = voltages.shape[0]
    inputs = local_inputs * chan_count
    spec_local = flags.shape[1]
    frame = voltages.shape[1] // spec_local
    history = taps.shape[0] - 1
    aligned = local_inputs % 128 == 0 and 128 % (4 * chan_count) == 0
    if aligned:
        own, tail = filterbank(voltages, taps, offsets, chan_count, spec_local)
    else:
        table = channel_table(frame, chan_count, 512, jnp.minimum(offsets[0], 0))
        own, tail = narrow_filterbank(voltages, taps, table, spec_local, 512, spec_local * local_inputs)
    earlier = lax.ppermute(tail, ("wide", "core"), [(i, i + 1) for i in range(time_count - 1)])
    spectrum = own + jnp.pad(earlier, ((0, 0), (0, spec_local - history), (0, 0)))
    flagged = (spectrum * flags.astype(jnp.float32).T[None]).astype(jnp.bfloat16)
    flagged = flagged.reshape(chan_count, 1, 2, spec_local, local_inputs)
    sent = jnp.broadcast_to(flagged, (chan_count, wide, 2, spec_local, local_inputs))
    sent = sent.reshape(chan_count * wide, 2, spec_local, local_inputs)
    mine = lax.all_to_all(sent, ("chan", "wide"), split_axis=0, concat_axis=0, tiled=True)
    other = lax.ppermute(mine, "core", [(0, 1), (1, 0)])
    shape = (chan_count, wide, 2, spec_local, local_inputs)
    mine, other = mine.reshape(shape), other.reshape(shape)
    scale = 1.0 / math.sqrt(spec_local * time_count)
    own_rows = inputs // time_count
    if aligned:
        return correlate((mine, other), offsets, scale, own_rows)[None]
    lanes = 256
    rows = [regroup(pieces, lanes) for pieces in (mine, other)]
    cols = [regroup(jnp.roll(pieces, -offsets[0], axis=0), lanes) for pieces in (mine, other)]
    return correlate((*rows, *cols), offsets * 0, scale, own_rows)[None]


def solution(mesh):
    devices = mesh.devices.reshape(mesh.shape["chan"], -1, 2)
    split = Mesh(devices, ("chan", "wide", "core"))
    time = ("wide", "core")
    in_specs = (P("chan", time), P(), P("chan", time), P("chan"))
    out_specs = P("chan", time, None, None)
    return jax.shard_map(shards, mesh=split, in_specs=in_specs, out_specs=out_specs, check_vma=False)
```

```python
import functools
import math

import jax
import jax.numpy as jnp
from jax import lax
from jax.experimental import pallas as pl
from jax.experimental.pallas import tpu as pltpu
from jax.sharding import Mesh
from jax.sharding import PartitionSpec as P

MIB = 1024 * 1024
ACROSS = (((1,), (1,)), ((), ()))
DOWN = (((0,), (0,)), ((), ()))
GROUP = 1
AHEAD = 3


def channel_table(frame, channels, width, shift):
    period = 4 * channels
    row = lax.broadcasted_iota(jnp.int32, (2 * channels, width), 0)
    sample = lax.broadcasted_iota(jnp.int32, (2 * channels, width), 1) + shift
    phase = (2 * (row // 2) + 1) * sample % period
    angle = phase.astype(jnp.float32) * (2.0 * math.pi / period)
    norm_scale = 1.0 / math.sqrt(frame)
    return jnp.where(row % 2 == 0, jnp.cos(angle), -jnp.sin(angle)) * norm_scale


def narrow_filterbank_kernel(spec, rows, taps, chunk, block, table, tap_ref, volt, own, tail, held, weights, total, sems):
    step, steps = pl.program_id(0), pl.num_programs(0)
    frame = steps * chunk
    pairs = table.shape[0]
    cols = taps * pairs

    def fetch(index, slot):
        for f in range(spec):
            pltpu.make_async_copy(
                volt.at[:, pl.ds(pl.multiple_of(f * frame + index * chunk, chunk), chunk)],
                held.at[slot, pl.ds(f * rows, rows), :],
                sems.at[slot, f],
            ).start()

    def arrive(slot):
        for f in range(spec):
            pltpu.make_async_copy(
                volt.at[:, pl.ds(0, chunk)], held.at[slot, pl.ds(f * rows, rows), :], sems.at[slot, f]
            ).wait()

    slot = lax.rem(step, 2)

    @pl.when(step == 0)
    def _():
        fetch(0, 0)
        total[...] = jnp.zeros_like(total)

    @pl.when(step + 1 < steps)
    def _():
        fetch(step + 1, 1 - slot)

    for t in range(taps):
        exact = tap_ref[t : t + 1, :] * table[...]
        high = exact.astype(jnp.bfloat16)
        low = (exact - high.astype(jnp.float32)).astype(jnp.bfloat16)
        weights[t * pairs : (t + 1) * pairs, :] = high
        weights[cols + t * pairs : cols + (t + 1) * pairs, :] = low

    arrive(slot)

    @pl.loop(0, spec * rows // block)
    def _(m):
        span = pl.ds(pl.multiple_of(m * block, block), block)
        total[span, :] += lax.dot_general(
            held[slot, span, :], weights[...], (((1,), (1,)), ((), ())), preferred_element_type=jnp.float32
        )

    @pl.when(step == steps - 1)
    def _():
        flipped = []
        for f in range(spec):
            part = total[f * rows : (f + 1) * rows, :]
            flipped.append((part[:, :cols] + part[:, cols:]).T)
        for f in range(spec + taps - 1):
            terms = [
                flipped[f - t][t * pairs : (t + 1) * pairs, :] for t in range(taps) if 0 <= f - t < spec
            ]
            value = functools.reduce(lambda a, b: a + b, terms)
            if f < spec:
                own[:, f, :] = value
            else:
                tail[:, f - spec, :] = value


def narrow_filterbank(volt, taps, table, spec, chunk, block):
    rows, width = volt.shape
    count, frame = taps.shape
    pairs = table.shape[0]
    cols = count * pairs
    return pl.pallas_call(
        functools.partial(narrow_filterbank_kernel, spec, rows, count, chunk, block),
        grid=(frame // chunk,),
        in_specs=[
            pl.BlockSpec((pairs, chunk), lambda s: (0, 0)),
            pl.BlockSpec((count, chunk), lambda s: (0, s)),
            pl.BlockSpec(memory_space=pl.ANY),
        ],
        out_specs=[
            pl.BlockSpec((pairs, spec, rows), lambda s: (0, 0, 0)),
            pl.BlockSpec((pairs, count - 1, rows), lambda s: (0, 0, 0)),
        ],
        out_shape=[
            jax.ShapeDtypeStruct((pairs, spec, rows), jnp.float32),
            jax.ShapeDtypeStruct((pairs, count - 1, rows), jnp.float32),
        ],
        scratch_shapes=[
            pltpu.VMEM((2, spec * rows, chunk), jnp.bfloat16),
            pltpu.VMEM((2 * cols, chunk), jnp.bfloat16),
            pltpu.VMEM((spec * rows, 2 * cols), jnp.float32),
            pltpu.SemaphoreType.DMA((2, spec)),
        ],
        compiler_params=pltpu.CompilerParams(vmem_limit_bytes=56 * MIB, dimension_semantics=("arbitrary",)),
        cost_estimate=pl.CostEstimate(
            flops=4 * spec * rows * frame * cols, bytes_accessed=2 * rows * width, transcendentals=0
        ),
    )(table, taps, volt)


def filterbank_kernel(spec, rows, offset, tap_hbm, volt, own, tail, tap_ref, held, weights, folded, sems, tap_sem):
    taps, frame = tap_ref.shape
    pairs = own.shape[0]
    cols = taps * pairs
    ring = held.shape[0]
    steps = spec // GROUP
    strip = 512

    def copies(step):
        slot = lax.rem(step, ring)
        made = []
        for n in range(GROUP):
            start = pl.multiple_of((step * GROUP + n) * frame, frame)
            made.append(
                pltpu.make_async_copy(
                    volt.at[:, pl.ds(start, frame)], held.at[slot, pl.ds(n * rows, rows), :], sems.at[slot]
                )
            )
        return made

    taps_copy = pltpu.make_async_copy(tap_hbm, tap_ref, tap_sem)
    taps_copy.start()

    @pl.loop(0, AHEAD)
    def _(step):
        for copy in copies(step):
            copy.start()

    folded[...] = jnp.zeros_like(folded)
    table = channel_table(frame, pairs // 2, 128, jnp.minimum(offset[0], 0))
    table = jnp.concatenate([table] * (strip // 128), axis=1)
    taps_copy.wait()

    @pl.loop(0, frame // strip)
    def _(s):
        span = pl.ds(pl.multiple_of(s * strip, strip), strip)
        for t in range(taps):
            exact = tap_ref[t : t + 1, span] * table
            high = exact.astype(jnp.bfloat16)
            low = (exact - high.astype(jnp.float32)).astype(jnp.bfloat16)
            weights[t * pairs : (t + 1) * pairs, span] = high
            weights[cols + t * pairs : cols + (t + 1) * pairs, span] = low

    @pl.loop(0, steps)
    def _(step):
        slot = lax.rem(step, ring)
        block = held.at[slot]
        pltpu.make_async_copy(block, block, sems.at[slot]).wait()

        @pl.when(step + AHEAD < steps)
        def _():
            for copy in copies(step + AHEAD):
                copy.start()

        value = lax.dot_general(weights[...], block[...], ACROSS, preferred_element_type=jnp.float32)
        value = value[:cols] + value[cols:]
        for t in range(taps):
            span = pl.ds(pl.multiple_of((step * GROUP + t) * rows, rows), GROUP * rows)
            folded[:, span] += value[t * pairs : (t + 1) * pairs, :]

    for f in range(spec + taps - 1):
        value = folded[:, f * rows : (f + 1) * rows]
        if f < spec:
            own[:, f, :] = value
        else:
            tail[:, f - spec, :] = value


def filterbank(volt, taps, offsets, channels, spec):
    rows, width = volt.shape
    count, frame = taps.shape
    pairs = 2 * channels
    cols = count * pairs
    return pl.pallas_call(
        functools.partial(filterbank_kernel, spec, rows),
        in_specs=[
            pl.BlockSpec(memory_space=pltpu.SMEM),
            pl.BlockSpec(memory_space=pltpu.HBM),
            pl.BlockSpec(memory_space=pltpu.HBM),
        ],
        out_specs=[pl.BlockSpec(memory_space=pltpu.VMEM)] * 2,
        out_shape=[
            jax.ShapeDtypeStruct((pairs, spec, rows), jnp.float32),
            jax.ShapeDtypeStruct((pairs, count - 1, rows), jnp.float32),
        ],
        scratch_shapes=[
            pltpu.VMEM((count, frame), jnp.float32),
            pltpu.VMEM((AHEAD + 1, GROUP * rows, frame), jnp.bfloat16),
            pltpu.VMEM((2 * cols, frame), jnp.bfloat16),
            pltpu.VMEM((pairs, (spec + count - 1) * rows), jnp.float32),
            pltpu.SemaphoreType.DMA((AHEAD + 1,)),
            pltpu.SemaphoreType.DMA,
        ],
        compiler_params=pltpu.CompilerParams(vmem_limit_bytes=107 * MIB // 2),
        cost_estimate=pl.CostEstimate(
            flops=4 * spec * rows * frame * cols, bytes_accessed=2 * rows * width, transcendentals=0
        ),
    )(offsets, taps, volt)


def correlate_kernel(scale, rotation, *refs):
    sources, (out, side, weave) = refs[:-3], refs[-3:]
    rows, columns = sources[:2], sources[-2:]
    blocks, wide, _, spec, lanes = columns[0].shape
    step = pl.program_id(0)

    @pl.when(step == 0)
    def _():
        for j in range(blocks):
            turned = lax.rem(j + rotation[0], blocks)
            at = 0
            for source in columns:
                for x in range(wide):
                    for part in range(2):
                        side[at : at + spec, j * lanes : (j + 1) * lanes] = source[turned, x, part]
                        at += spec
        taken = lax.broadcasted_iota(jnp.int32, weave.shape, 0)
        made = lax.broadcasted_iota(jnp.int32, weave.shape, 1)
        weave[...] = (taken == made // 2 + made % 2 * lanes).astype(jnp.float32).astype(jnp.bfloat16)

    place = (lax.axis_index("wide") * 2 + lax.axis_index("core")) * pl.num_programs(0) + step
    real, imag = [], []
    for source in rows:
        for x in range(wide):
            first, second = source[place, x, 0], source[place, x, 1]
            real += [first, second]
            imag += [second, -first]
    both = jnp.concatenate([jnp.concatenate(real, axis=0), jnp.concatenate(imag, axis=0)], axis=1)
    woven = jnp.dot(both, weave[...], preferred_element_type=jnp.float32)
    exact = math.frexp(scale)[0] == 0.5
    if exact:
        woven *= scale
    value = lax.dot_general(woven.astype(jnp.bfloat16), side[...], DOWN, preferred_element_type=jnp.float32)
    if not exact:
        value *= scale
    out[...] = value.astype(jnp.bfloat16).reshape(out.shape)


def correlate(sources, rotation, scale, own_rows):
    blocks, wide, parts, spec, lanes = sources[0].shape
    whole = pl.BlockSpec(memory_space=pltpu.VMEM)
    return pl.pallas_call(
        functools.partial(correlate_kernel, scale),
        grid_spec=pltpu.PrefetchScalarGridSpec(
            num_scalar_prefetch=1,
            grid=(own_rows // lanes,),
            in_specs=[whole] * len(sources),
            out_specs=pl.BlockSpec((lanes, 2, blocks * lanes), lambda i, rotation: (i, 0, 0)),
            scratch_shapes=[
                pltpu.VMEM((2 * wide * 2 * spec, blocks * lanes), jnp.bfloat16),
                pltpu.VMEM((2 * lanes, 2 * lanes), jnp.bfloat16),
            ],
        ),
        out_shape=jax.ShapeDtypeStruct((own_rows, 2, blocks * lanes), jnp.bfloat16),
        compiler_params=pltpu.CompilerParams(vmem_limit_bytes=24 * MIB, dimension_semantics=("arbitrary",)),
    )(rotation, *sources)


def regroup(pieces, lanes):
    blocks, wide, parts, spec, narrow = pieces.shape
    join = lanes // narrow
    pieces = pieces.reshape(blocks // join, join, wide, parts, spec, narrow)
    return jnp.transpose(pieces, (0, 2, 3, 4, 1, 5)).reshape(blocks // join, wide, parts, spec, lanes)


def shards(voltages, taps, flags, offsets):
    chan_count, wide, cores = (lax.axis_size(name) for name in ("chan", "wide", "core"))
    time_count = wide * cores
    local_inputs = voltages.shape[0]
    inputs = local_inputs * chan_count
    spec_local = flags.shape[1]
    frame = voltages.shape[1] // spec_local
    history = taps.shape[0] - 1
    aligned = local_inputs % 128 == 0 and 128 % (4 * chan_count) == 0
    if aligned:
        own, tail = filterbank(voltages, taps, offsets, chan_count, spec_local)
    else:
        table = channel_table(frame, chan_count, 512, jnp.minimum(offsets[0], 0))
        own, tail = narrow_filterbank(voltages, taps, table, spec_local, 512, spec_local * local_inputs)
    earlier = lax.ppermute(tail, ("wide", "core"), [(i, i + 1) for i in range(time_count - 1)])
    spectrum = own + jnp.pad(earlier, ((0, 0), (0, spec_local - history), (0, 0)))
    flagged = (spectrum * flags.astype(jnp.float32).T[None]).astype(jnp.bfloat16)
    flagged = flagged.reshape(chan_count, 1, 2, spec_local, local_inputs)
    sent = jnp.broadcast_to(flagged, (chan_count, wide, 2, spec_local, local_inputs))
    sent = sent.reshape(chan_count * wide, 2, spec_local, local_inputs)
    mine = lax.all_to_all(sent, ("chan", "wide"), split_axis=0, concat_axis=0, tiled=True)
    other = lax.ppermute(mine, "core", [(0, 1), (1, 0)])
    shape = (chan_count, wide, 2, spec_local, local_inputs)
    mine, other = mine.reshape(shape), other.reshape(shape)
    scale = 1.0 / math.sqrt(spec_local * time_count)
    own_rows = inputs // time_count
    if aligned:
        return correlate((mine, other), offsets, scale, own_rows)[None]
    lanes = 256
    rows = [regroup(pieces, lanes) for pieces in (mine, other)]
    cols = [regroup(jnp.roll(pieces, -offsets[0], axis=0), lanes) for pieces in (mine, other)]
    return correlate((*rows, *cols), offsets * 0, scale, own_rows)[None]


def solution(mesh):
    devices = mesh.devices.reshape(mesh.shape["chan"], -1, 2)
    split = Mesh(devices, ("chan", "wide", "core"))
    time = ("wide", "core")
    in_specs = (P("chan", time), P(), P("chan", time), P("chan"))
    out_specs = P("chan", time, None, None)
    return jax.shard_map(shards, mesh=split, in_specs=in_specs, out_specs=out_specs, check_vma=False)
```

```python
import functools
import math

import jax
import jax.numpy as jnp
from jax import lax
from jax.experimental import pallas as pl
from jax.experimental.pallas import tpu as pltpu
from jax.sharding import Mesh
from jax.sharding import PartitionSpec as P

MIB = 1024 * 1024
ACROSS = (((1,), (1,)), ((), ()))
DOWN = (((0,), (0,)), ((), ()))
AHEAD = 3
READY = 2
LATE = 9


def channel_table(frame, channels, width, shift):
    period = 4 * channels
    row = lax.broadcasted_iota(jnp.int32, (2 * channels, width), 0)
    sample = lax.broadcasted_iota(jnp.int32, (2 * channels, width), 1) + shift
    phase = (2 * (row // 2) + 1) * sample % period
    angle = phase.astype(jnp.float32) * (2.0 * math.pi / period)
    norm_scale = 1.0 / math.sqrt(frame)
    return jnp.where(row % 2 == 0, jnp.cos(angle), -jnp.sin(angle)) * norm_scale


def narrow_filterbank_kernel(spec, rows, taps, chunk, block, table, tap_ref, volt, own, tail, held, weights, total, sems):
    step, steps = pl.program_id(0), pl.num_programs(0)
    frame = steps * chunk
    pairs = table.shape[0]
    cols = taps * pairs

    def fetch(index, slot):
        for f in range(spec):
            pltpu.make_async_copy(
                volt.at[:, pl.ds(pl.multiple_of(f * frame + index * chunk, chunk), chunk)],
                held.at[slot, pl.ds(f * rows, rows), :],
                sems.at[slot, f],
            ).start()

    def arrive(slot):
        for f in range(spec):
            pltpu.make_async_copy(
                volt.at[:, pl.ds(0, chunk)], held.at[slot, pl.ds(f * rows, rows), :], sems.at[slot, f]
            ).wait()

    slot = lax.rem(step, 2)

    @pl.when(step == 0)
    def _():
        fetch(0, 0)
        total[...] = jnp.zeros_like(total)

    @pl.when(step + 1 < steps)
    def _():
        fetch(step + 1, 1 - slot)

    for t in range(taps):
        exact = tap_ref[t : t + 1, :] * table[...]
        high = exact.astype(jnp.bfloat16)
        low = (exact - high.astype(jnp.float32)).astype(jnp.bfloat16)
        weights[t * pairs : (t + 1) * pairs, :] = high
        weights[cols + t * pairs : cols + (t + 1) * pairs, :] = low

    arrive(slot)

    @pl.loop(0, spec * rows // block)
    def _(m):
        span = pl.ds(pl.multiple_of(m * block, block), block)
        total[span, :] += lax.dot_general(
            held[slot, span, :], weights[...], (((1,), (1,)), ((), ())), preferred_element_type=jnp.float32
        )

    @pl.when(step == steps - 1)
    def _():
        flipped = []
        for f in range(spec):
            part = total[f * rows : (f + 1) * rows, :]
            flipped.append((part[:, :cols] + part[:, cols:]).T)
        for f in range(spec + taps - 1):
            terms = [
                flipped[f - t][t * pairs : (t + 1) * pairs, :] for t in range(taps) if 0 <= f - t < spec
            ]
            value = functools.reduce(lambda a, b: a + b, terms)
            if f < spec:
                own[:, f, :] = value
            else:
                tail[:, f - spec, :] = value


def narrow_filterbank(volt, taps, table, spec, chunk, block):
    rows, width = volt.shape
    count, frame = taps.shape
    pairs = table.shape[0]
    cols = count * pairs
    return pl.pallas_call(
        functools.partial(narrow_filterbank_kernel, spec, rows, count, chunk, block),
        grid=(frame // chunk,),
        in_specs=[
            pl.BlockSpec((pairs, chunk), lambda s: (0, 0)),
            pl.BlockSpec((count, chunk), lambda s: (0, s)),
            pl.BlockSpec(memory_space=pl.ANY),
        ],
        out_specs=[
            pl.BlockSpec((pairs, spec, rows), lambda s: (0, 0, 0)),
            pl.BlockSpec((pairs, count - 1, rows), lambda s: (0, 0, 0)),
        ],
        out_shape=[
            jax.ShapeDtypeStruct((pairs, spec, rows), jnp.float32),
            jax.ShapeDtypeStruct((pairs, count - 1, rows), jnp.float32),
        ],
        scratch_shapes=[
            pltpu.VMEM((2, spec * rows, chunk), jnp.bfloat16),
            pltpu.VMEM((2 * cols, chunk), jnp.bfloat16),
            pltpu.VMEM((spec * rows, 2 * cols), jnp.float32),
            pltpu.SemaphoreType.DMA((2, spec)),
        ],
        compiler_params=pltpu.CompilerParams(vmem_limit_bytes=56 * MIB, dimension_semantics=("arbitrary",)),
        cost_estimate=pl.CostEstimate(
            flops=4 * spec * rows * frame * cols, bytes_accessed=2 * rows * width, transcendentals=0
        ),
    )(table, taps, volt)


def frame_copy(volt, f, target, sem):
    frame = target.shape[-1]
    return pltpu.make_async_copy(volt.at[:, pl.ds(pl.multiple_of(f * frame, frame), frame)], target, sem)


def add_frame(weights, block, folded, f, pairs):
    value = lax.dot_general(weights[...], block[...], ACROSS, preferred_element_type=jnp.float32)
    rows = value.shape[1]
    cols = value.shape[0] // 2
    value = value[:cols] + value[cols:]
    for t in range(cols // pairs):
        span = pl.ds(pl.multiple_of((f + t) * rows, rows), rows)
        folded[:, span] += value[t * pairs : (t + 1) * pairs, :]


def late_kernel(spec, rows, offset, tap_ref, volt, tail, partial, weights, ready, held, folded, sems, ready_sems):
    taps, frame = tap_ref.shape
    pairs = partial.shape[0]
    cols = taps * pairs
    ring = held.shape[0]
    first, count, history = spec - LATE, LATE, taps - 1
    strip = 512

    def start(step):
        @pl.when(step < count)
        def _():
            slot = lax.rem(step, ring)
            frame_copy(volt, first + step, held.at[slot], sems.at[slot]).start()

        @pl.when((step >= count) & (step < count + READY))
        def _():
            f = step - count
            frame_copy(volt, f, ready.at[f], ready_sems.at[f]).start()

    strips = frame // strip
    stage = strips // (AHEAD - 1)
    start(jnp.int32(0))
    folded[...] = jnp.zeros_like(folded)
    table = channel_table(frame, pairs // 2, 128, jnp.minimum(offset[0], 0))
    table = jnp.concatenate([table] * (strip // 128), axis=1)

    @pl.loop(0, strips)
    def _(s):
        @pl.when(lax.rem(s + 1, stage) == 0)
        def _():
            start((s + 1) // stage)

        span = pl.ds(pl.multiple_of(s * strip, strip), strip)
        for t in range(taps):
            exact = tap_ref[t : t + 1, span] * table
            high = exact.astype(jnp.bfloat16)
            low = (exact - high.astype(jnp.float32)).astype(jnp.bfloat16)
            weights[t * pairs : (t + 1) * pairs, span] = high
            weights[cols + t * pairs : cols + (t + 1) * pairs, span] = low

    @pl.loop(0, count)
    def _(step):
        slot = lax.rem(step, ring)
        pltpu.make_async_copy(held.at[slot], held.at[slot], sems.at[slot]).wait()
        start(step + AHEAD)
        add_frame(weights, held.at[slot], folded, first + step, pairs)

    for f in range(history):
        tail[:, f, :] = folded[:, (spec + f) * rows : (spec + f + 1) * rows]
    partial[...] = folded[:, : spec * rows]

    for f in range(READY):
        pltpu.make_async_copy(ready.at[f], ready.at[f], ready_sems.at[f]).wait()


def early_kernel(spec, rows, weights, ready, partial, volt, own, held, folded, sems):
    frame = weights.shape[1]
    pairs = partial.shape[0]
    ring = held.shape[0]
    count = spec - LATE - READY

    def start(step):
        @pl.when(step < count)
        def _():
            slot = lax.rem(step, ring)
            frame_copy(volt, READY + step, held.at[slot], sems.at[slot]).start()

    @pl.loop(0, AHEAD)
    def _(step):
        start(step)

    folded[...] = partial[...]

    @pl.loop(0, READY)
    def _(f):
        add_frame(weights, ready.at[f], folded, f, pairs)

    @pl.loop(0, count)
    def _(step):
        slot = lax.rem(step, ring)
        pltpu.make_async_copy(held.at[slot], held.at[slot], sems.at[slot]).wait()
        start(step + AHEAD)
        add_frame(weights, held.at[slot], folded, READY + step, pairs)

    for f in range(spec):
        own[:, f, :] = folded[:, f * rows : (f + 1) * rows]


def filterbank(volt, taps, offsets, channels, spec):
    rows, width = volt.shape
    count, frame = taps.shape
    pairs = 2 * channels
    cols = count * pairs
    vmem, hbm = pl.BlockSpec(memory_space=pltpu.VMEM), pl.BlockSpec(memory_space=pl.ANY)

    def cost(frames):
        return pl.CostEstimate(
            flops=4 * frames * rows * frame * cols, bytes_accessed=2 * frames * rows * frame, transcendentals=0
        )

    tail, partial, weights, ready = pl.pallas_call(
        functools.partial(late_kernel, spec, rows),
        in_specs=[pl.BlockSpec(memory_space=pltpu.SMEM), vmem, hbm],
        out_specs=[vmem] * 4,
        out_shape=[
            jax.ShapeDtypeStruct((pairs, count - 1, rows), jnp.float32),
            jax.ShapeDtypeStruct((pairs, spec * rows), jnp.float32),
            jax.ShapeDtypeStruct((2 * cols, frame), jnp.bfloat16),
            jax.ShapeDtypeStruct((READY, rows, frame), jnp.bfloat16),
        ],
        scratch_shapes=[
            pltpu.VMEM((AHEAD + 1, rows, frame), jnp.bfloat16),
            pltpu.VMEM((pairs, (spec + count - 1) * rows), jnp.float32),
            pltpu.SemaphoreType.DMA((AHEAD + 1,)),
            pltpu.SemaphoreType.DMA((READY,)),
        ],
        compiler_params=pltpu.CompilerParams(vmem_limit_bytes=24 * MIB),
        cost_estimate=cost(LATE),
    )(offsets, taps, volt)
    own = pl.pallas_call(
        functools.partial(early_kernel, spec, rows),
        in_specs=[vmem, vmem, vmem, hbm],
        out_specs=vmem,
        out_shape=jax.ShapeDtypeStruct((pairs, spec, rows), jnp.float32),
        scratch_shapes=[
            pltpu.VMEM((AHEAD + 1, rows, frame), jnp.bfloat16),
            pltpu.VMEM((pairs, spec * rows), jnp.float32),
            pltpu.SemaphoreType.DMA((AHEAD + 1,)),
        ],
        compiler_params=pltpu.CompilerParams(vmem_limit_bytes=24 * MIB),
        cost_estimate=cost(spec - LATE),
    )(weights, ready, partial, volt)
    return own, tail


def correlate_kernel(scale, rotation, *refs):
    sources, (out, side, weave) = refs[:-3], refs[-3:]
    rows, columns = sources[:2], sources[-2:]
    blocks, wide, _, spec, lanes = columns[0].shape
    step = pl.program_id(0)

    @pl.when(step == 0)
    def _():
        for j in range(blocks):
            turned = lax.rem(j + rotation[0], blocks)
            at = 0
            for source in columns:
                for x in range(wide):
                    for part in range(2):
                        side[at : at + spec, j * lanes : (j + 1) * lanes] = source[turned, x, part]
                        at += spec
        taken = lax.broadcasted_iota(jnp.int32, weave.shape, 0)
        made = lax.broadcasted_iota(jnp.int32, weave.shape, 1)
        weave[...] = (taken == made // 2 + made % 2 * lanes).astype(jnp.float32).astype(jnp.bfloat16)

    place = (lax.axis_index("wide") * 2 + lax.axis_index("core")) * pl.num_programs(0) + step
    real, imag = [], []
    for source in rows:
        for x in range(wide):
            first, second = source[place, x, 0], source[place, x, 1]
            real += [first, second]
            imag += [second, -first]
    both = jnp.concatenate([jnp.concatenate(real, axis=0), jnp.concatenate(imag, axis=0)], axis=1)
    woven = jnp.dot(both, weave[...], preferred_element_type=jnp.float32)
    exact = math.frexp(scale)[0] == 0.5
    if exact:
        woven *= scale
    value = lax.dot_general(woven.astype(jnp.bfloat16), side[...], DOWN, preferred_element_type=jnp.float32)
    if not exact:
        value *= scale
    out[...] = value.astype(jnp.bfloat16).reshape(out.shape)


def correlate(sources, rotation, scale, own_rows):
    blocks, wide, parts, spec, lanes = sources[0].shape
    whole = pl.BlockSpec(memory_space=pltpu.VMEM)
    return pl.pallas_call(
        functools.partial(correlate_kernel, scale),
        grid_spec=pltpu.PrefetchScalarGridSpec(
            num_scalar_prefetch=1,
            grid=(own_rows // lanes,),
            in_specs=[whole] * len(sources),
            out_specs=pl.BlockSpec((lanes, 2, blocks * lanes), lambda i, rotation: (i, 0, 0)),
            scratch_shapes=[
                pltpu.VMEM((2 * wide * 2 * spec, blocks * lanes), jnp.bfloat16),
                pltpu.VMEM((2 * lanes, 2 * lanes), jnp.bfloat16),
            ],
        ),
        out_shape=jax.ShapeDtypeStruct((own_rows, 2, blocks * lanes), jnp.bfloat16),
        compiler_params=pltpu.CompilerParams(vmem_limit_bytes=24 * MIB, dimension_semantics=("arbitrary",)),
    )(rotation, *sources)


def regroup(pieces, lanes):
    blocks, wide, parts, spec, narrow = pieces.shape
    join = lanes // narrow
    pieces = pieces.reshape(blocks // join, join, wide, parts, spec, narrow)
    return jnp.transpose(pieces, (0, 2, 3, 4, 1, 5)).reshape(blocks // join, wide, parts, spec, lanes)


def shards(voltages, taps, flags, offsets):
    chan_count, wide, cores = (lax.axis_size(name) for name in ("chan", "wide", "core"))
    time_count = wide * cores
    local_inputs = voltages.shape[0]
    inputs = local_inputs * chan_count
    spec_local = flags.shape[1]
    frame = voltages.shape[1] // spec_local
    history = taps.shape[0] - 1
    aligned = local_inputs % 128 == 0 and 128 % (4 * chan_count) == 0
    if aligned:
        own, tail = filterbank(voltages, taps, offsets, chan_count, spec_local)
    else:
        table = channel_table(frame, chan_count, 512, jnp.minimum(offsets[0], 0))
        own, tail = narrow_filterbank(voltages, taps, table, spec_local, 512, spec_local * local_inputs)
    earlier = lax.ppermute(tail, ("wide", "core"), [(i, i + 1) for i in range(time_count - 1)])
    spectrum = own + jnp.pad(earlier, ((0, 0), (0, spec_local - history), (0, 0)))
    flagged = (spectrum * flags.astype(jnp.float32).T[None]).astype(jnp.bfloat16)
    flagged = flagged.reshape(chan_count, 1, 2, spec_local, local_inputs)
    sent = jnp.broadcast_to(flagged, (chan_count, wide, 2, spec_local, local_inputs))
    sent = sent.reshape(chan_count * wide, 2, spec_local, local_inputs)
    mine = lax.all_to_all(sent, ("chan", "wide"), split_axis=0, concat_axis=0, tiled=True)
    other = lax.ppermute(mine, "core", [(0, 1), (1, 0)])
    shape = (chan_count, wide, 2, spec_local, local_inputs)
    mine, other = mine.reshape(shape), other.reshape(shape)
    scale = 1.0 / math.sqrt(spec_local * time_count)
    own_rows = inputs // time_count
    if aligned:
        return correlate((mine, other), offsets, scale, own_rows)[None]
    lanes = 256
    rows = [regroup(pieces, lanes) for pieces in (mine, other)]
    cols = [regroup(jnp.roll(pieces, -offsets[0], axis=0), lanes) for pieces in (mine, other)]
    return correlate((*rows, *cols), offsets * 0, scale, own_rows)[None]


def solution(mesh):
    devices = mesh.devices.reshape(mesh.shape["chan"], -1, 2)
    split = Mesh(devices, ("chan", "wide", "core"))
    time = ("wide", "core")
    in_specs = (P("chan", time), P(), P("chan", time), P("chan"))
    out_specs = P("chan", time, None, None)
    return jax.shard_map(shards, mesh=split, in_specs=in_specs, out_specs=out_specs, check_vma=False)
```

```python
import functools
import math

import jax
import jax.numpy as jnp
from jax import lax
from jax.experimental import pallas as pl
from jax.experimental.pallas import tpu as pltpu
from jax.sharding import Mesh
from jax.sharding import PartitionSpec as P

MIB = 1024 * 1024
ACROSS = (((1,), (1,)), ((), ()))
DOWN = (((0,), (0,)), ((), ()))
AHEAD = 3
READY = 2
LATE = 10


def channel_table(frame, channels, width, shift):
    period = 4 * channels
    row = lax.broadcasted_iota(jnp.int32, (2 * channels, width), 0)
    sample = lax.broadcasted_iota(jnp.int32, (2 * channels, width), 1) + shift
    phase = (2 * (row // 2) + 1) * sample % period
    angle = phase.astype(jnp.float32) * (2.0 * math.pi / period)
    norm_scale = 1.0 / math.sqrt(frame)
    return jnp.where(row % 2 == 0, jnp.cos(angle), -jnp.sin(angle)) * norm_scale


def narrow_filterbank_kernel(spec, rows, taps, chunk, block, table, tap_ref, volt, own, tail, held, weights, total, sems):
    step, steps = pl.program_id(0), pl.num_programs(0)
    frame = steps * chunk
    pairs = table.shape[0]
    cols = taps * pairs

    def fetch(index, slot):
        for f in range(spec):
            pltpu.make_async_copy(
                volt.at[:, pl.ds(pl.multiple_of(f * frame + index * chunk, chunk), chunk)],
                held.at[slot, pl.ds(f * rows, rows), :],
                sems.at[slot, f],
            ).start()

    def arrive(slot):
        for f in range(spec):
            pltpu.make_async_copy(
                volt.at[:, pl.ds(0, chunk)], held.at[slot, pl.ds(f * rows, rows), :], sems.at[slot, f]
            ).wait()

    slot = lax.rem(step, 2)

    @pl.when(step == 0)
    def _():
        fetch(0, 0)
        total[...] = jnp.zeros_like(total)

    @pl.when(step + 1 < steps)
    def _():
        fetch(step + 1, 1 - slot)

    for t in range(taps):
        exact = tap_ref[t : t + 1, :] * table[...]
        high = exact.astype(jnp.bfloat16)
        low = (exact - high.astype(jnp.float32)).astype(jnp.bfloat16)
        weights[t * pairs : (t + 1) * pairs, :] = high
        weights[cols + t * pairs : cols + (t + 1) * pairs, :] = low

    arrive(slot)

    @pl.loop(0, spec * rows // block)
    def _(m):
        span = pl.ds(pl.multiple_of(m * block, block), block)
        total[span, :] += lax.dot_general(
            held[slot, span, :], weights[...], (((1,), (1,)), ((), ())), preferred_element_type=jnp.float32
        )

    @pl.when(step == steps - 1)
    def _():
        flipped = []
        for f in range(spec):
            part = total[f * rows : (f + 1) * rows, :]
            flipped.append((part[:, :cols] + part[:, cols:]).T)
        for f in range(spec + taps - 1):
            terms = [
                flipped[f - t][t * pairs : (t + 1) * pairs, :] for t in range(taps) if 0 <= f - t < spec
            ]
            value = functools.reduce(lambda a, b: a + b, terms)
            if f < spec:
                own[:, f, :] = value
            else:
                tail[:, f - spec, :] = value


def narrow_filterbank(volt, taps, table, spec, chunk, block):
    rows, width = volt.shape
    count, frame = taps.shape
    pairs = table.shape[0]
    cols = count * pairs
    return pl.pallas_call(
        functools.partial(narrow_filterbank_kernel, spec, rows, count, chunk, block),
        grid=(frame // chunk,),
        in_specs=[
            pl.BlockSpec((pairs, chunk), lambda s: (0, 0)),
            pl.BlockSpec((count, chunk), lambda s: (0, s)),
            pl.BlockSpec(memory_space=pl.ANY),
        ],
        out_specs=[
            pl.BlockSpec((pairs, spec, rows), lambda s: (0, 0, 0)),
            pl.BlockSpec((pairs, count - 1, rows), lambda s: (0, 0, 0)),
        ],
        out_shape=[
            jax.ShapeDtypeStruct((pairs, spec, rows), jnp.float32),
            jax.ShapeDtypeStruct((pairs, count - 1, rows), jnp.float32),
        ],
        scratch_shapes=[
            pltpu.VMEM((2, spec * rows, chunk), jnp.bfloat16),
            pltpu.VMEM((2 * cols, chunk), jnp.bfloat16),
            pltpu.VMEM((spec * rows, 2 * cols), jnp.float32),
            pltpu.SemaphoreType.DMA((2, spec)),
        ],
        compiler_params=pltpu.CompilerParams(vmem_limit_bytes=56 * MIB, dimension_semantics=("arbitrary",)),
        cost_estimate=pl.CostEstimate(
            flops=4 * spec * rows * frame * cols, bytes_accessed=2 * rows * width, transcendentals=0
        ),
    )(table, taps, volt)


def frame_copy(volt, f, target, sem):
    frame = target.shape[-1]
    return pltpu.make_async_copy(volt.at[:, pl.ds(pl.multiple_of(f * frame, frame), frame)], target, sem)


def add_frame(weights, block, folded, f, pairs):
    value = lax.dot_general(weights[...], block[...], ACROSS, preferred_element_type=jnp.float32)
    rows = value.shape[1]
    cols = value.shape[0] // 2
    value = value[:cols] + value[cols:]
    for t in range(cols // pairs):
        span = pl.ds(pl.multiple_of((f + t) * rows, rows), rows)
        folded[:, span] += value[t * pairs : (t + 1) * pairs, :]


def late_kernel(spec, rows, offset, tap_ref, volt, tail, partial, weights, ready, held, folded, sems, ready_sems):
    taps, frame = tap_ref.shape
    pairs = partial.shape[0]
    cols = taps * pairs
    ring = held.shape[0]
    first, count, history = spec - LATE, LATE, taps - 1
    strip = 512

    def start(step):
        @pl.when(step < count)
        def _():
            slot = lax.rem(step, ring)
            frame_copy(volt, first + step, held.at[slot], sems.at[slot]).start()

        @pl.when((step >= count) & (step < count + READY))
        def _():
            f = step - count
            frame_copy(volt, f, ready.at[f], ready_sems.at[f]).start()

    strips = frame // strip
    stage = strips // (AHEAD - 1)
    start(jnp.int32(0))
    folded[...] = jnp.zeros_like(folded)
    table = channel_table(frame, pairs // 2, 128, jnp.minimum(offset[0], 0))
    table = jnp.concatenate([table] * (strip // 128), axis=1)

    @pl.loop(0, strips)
    def _(s):
        @pl.when(lax.rem(s + 1, stage) == 0)
        def _():
            start((s + 1) // stage)

        span = pl.ds(pl.multiple_of(s * strip, strip), strip)
        for t in range(taps):
            exact = tap_ref[t : t + 1, span] * table
            high = exact.astype(jnp.bfloat16)
            low = (exact - high.astype(jnp.float32)).astype(jnp.bfloat16)
            weights[t * pairs : (t + 1) * pairs, span] = high
            weights[cols + t * pairs : cols + (t + 1) * pairs, span] = low

    @pl.loop(0, count)
    def _(step):
        slot = lax.rem(step, ring)
        pltpu.make_async_copy(held.at[slot], held.at[slot], sems.at[slot]).wait()
        start(step + AHEAD)
        add_frame(weights, held.at[slot], folded, first + step, pairs)

    for f in range(history):
        tail[:, f, :] = folded[:, (spec + f) * rows : (spec + f + 1) * rows]
    partial[...] = folded[:, : spec * rows]

    for f in range(READY):
        pltpu.make_async_copy(ready.at[f], ready.at[f], ready_sems.at[f]).wait()


def early_kernel(spec, rows, weights, ready, partial, volt, own, held, folded, sems):
    frame = weights.shape[1]
    pairs = partial.shape[0]
    ring = held.shape[0]
    count = spec - LATE - READY

    def start(step):
        @pl.when(step < count)
        def _():
            slot = lax.rem(step, ring)
            frame_copy(volt, READY + step, held.at[slot], sems.at[slot]).start()

    @pl.loop(0, AHEAD)
    def _(step):
        start(step)

    folded[...] = partial[...]

    @pl.loop(0, READY)
    def _(f):
        add_frame(weights, ready.at[f], folded, f, pairs)

    @pl.loop(0, count)
    def _(step):
        slot = lax.rem(step, ring)
        pltpu.make_async_copy(held.at[slot], held.at[slot], sems.at[slot]).wait()
        start(step + AHEAD)
        add_frame(weights, held.at[slot], folded, READY + step, pairs)

    for f in range(spec):
        own[:, f, :] = folded[:, f * rows : (f + 1) * rows]


def filterbank(volt, taps, offsets, channels, spec):
    rows, width = volt.shape
    count, frame = taps.shape
    pairs = 2 * channels
    cols = count * pairs
    vmem, hbm = pl.BlockSpec(memory_space=pltpu.VMEM), pl.BlockSpec(memory_space=pl.ANY)

    def cost(frames):
        return pl.CostEstimate(
            flops=4 * frames * rows * frame * cols, bytes_accessed=2 * frames * rows * frame, transcendentals=0
        )

    tail, partial, weights, ready = pl.pallas_call(
        functools.partial(late_kernel, spec, rows),
        in_specs=[pl.BlockSpec(memory_space=pltpu.SMEM), vmem, hbm],
        out_specs=[vmem] * 4,
        out_shape=[
            jax.ShapeDtypeStruct((pairs, count - 1, rows), jnp.float32),
            jax.ShapeDtypeStruct((pairs, spec * rows), jnp.float32),
            jax.ShapeDtypeStruct((2 * cols, frame), jnp.bfloat16),
            jax.ShapeDtypeStruct((READY, rows, frame), jnp.bfloat16),
        ],
        scratch_shapes=[
            pltpu.VMEM((AHEAD + 1, rows, frame), jnp.bfloat16),
            pltpu.VMEM((pairs, (spec + count - 1) * rows), jnp.float32),
            pltpu.SemaphoreType.DMA((AHEAD + 1,)),
            pltpu.SemaphoreType.DMA((READY,)),
        ],
        compiler_params=pltpu.CompilerParams(vmem_limit_bytes=24 * MIB),
        cost_estimate=cost(LATE),
    )(offsets, taps, volt)
    own = pl.pallas_call(
        functools.partial(early_kernel, spec, rows),
        in_specs=[vmem, vmem, vmem, hbm],
        out_specs=vmem,
        out_shape=jax.ShapeDtypeStruct((pairs, spec, rows), jnp.float32),
        scratch_shapes=[
            pltpu.VMEM((AHEAD + 1, rows, frame), jnp.bfloat16),
            pltpu.VMEM((pairs, spec * rows), jnp.float32),
            pltpu.SemaphoreType.DMA((AHEAD + 1,)),
        ],
        compiler_params=pltpu.CompilerParams(vmem_limit_bytes=24 * MIB),
        cost_estimate=cost(spec - LATE),
    )(weights, ready, partial, volt)
    return own, tail


def correlate_kernel(scale, rotation, *refs):
    sources, (out, side, weave) = refs[:-3], refs[-3:]
    rows, columns = sources[:2], sources[-2:]
    blocks, wide, _, spec, lanes = columns[0].shape
    step = pl.program_id(0)

    @pl.when(step == 0)
    def _():
        for j in range(blocks):
            turned = lax.rem(j + rotation[0], blocks)
            at = 0
            for source in columns:
                for x in range(wide):
                    for part in range(2):
                        side[at : at + spec, j * lanes : (j + 1) * lanes] = source[turned, x, part]
                        at += spec
        taken = lax.broadcasted_iota(jnp.int32, weave.shape, 0)
        made = lax.broadcasted_iota(jnp.int32, weave.shape, 1)
        weave[...] = (taken == made // 2 + made % 2 * lanes).astype(jnp.float32).astype(jnp.bfloat16)

    place = (lax.axis_index("wide") * 2 + lax.axis_index("core")) * pl.num_programs(0) + step
    real, imag = [], []
    for source in rows:
        for x in range(wide):
            first, second = source[place, x, 0], source[place, x, 1]
            real += [first, second]
            imag += [second, -first]
    both = jnp.concatenate([jnp.concatenate(real, axis=0), jnp.concatenate(imag, axis=0)], axis=1)
    woven = jnp.dot(both, weave[...], preferred_element_type=jnp.float32)
    exact = math.frexp(scale)[0] == 0.5
    if exact:
        woven *= scale
    value = lax.dot_general(woven.astype(jnp.bfloat16), side[...], DOWN, preferred_element_type=jnp.float32)
    if not exact:
        value *= scale
    out[...] = value.astype(jnp.bfloat16).reshape(out.shape)


def correlate(sources, rotation, scale, own_rows):
    blocks, wide, parts, spec, lanes = sources[0].shape
    whole = pl.BlockSpec(memory_space=pltpu.VMEM)
    return pl.pallas_call(
        functools.partial(correlate_kernel, scale),
        grid_spec=pltpu.PrefetchScalarGridSpec(
            num_scalar_prefetch=1,
            grid=(own_rows // lanes,),
            in_specs=[whole] * len(sources),
            out_specs=pl.BlockSpec((lanes, 2, blocks * lanes), lambda i, rotation: (i, 0, 0)),
            scratch_shapes=[
                pltpu.VMEM((2 * wide * 2 * spec, blocks * lanes), jnp.bfloat16),
                pltpu.VMEM((2 * lanes, 2 * lanes), jnp.bfloat16),
            ],
        ),
        out_shape=jax.ShapeDtypeStruct((own_rows, 2, blocks * lanes), jnp.bfloat16),
        compiler_params=pltpu.CompilerParams(vmem_limit_bytes=24 * MIB, dimension_semantics=("arbitrary",)),
    )(rotation, *sources)


def regroup(pieces, lanes):
    blocks, wide, parts, spec, narrow = pieces.shape
    join = lanes // narrow
    pieces = pieces.reshape(blocks // join, join, wide, parts, spec, narrow)
    return jnp.transpose(pieces, (0, 2, 3, 4, 1, 5)).reshape(blocks // join, wide, parts, spec, lanes)


def shards(voltages, taps, flags, offsets):
    chan_count, wide, cores = (lax.axis_size(name) for name in ("chan", "wide", "core"))
    time_count = wide * cores
    local_inputs = voltages.shape[0]
    inputs = local_inputs * chan_count
    spec_local = flags.shape[1]
    frame = voltages.shape[1] // spec_local
    history = taps.shape[0] - 1
    aligned = local_inputs % 128 == 0 and 128 % (4 * chan_count) == 0
    if aligned:
        own, tail = filterbank(voltages, taps, offsets, chan_count, spec_local)
    else:
        table = channel_table(frame, chan_count, 512, jnp.minimum(offsets[0], 0))
        own, tail = narrow_filterbank(voltages, taps, table, spec_local, 512, spec_local * local_inputs)
    earlier = lax.ppermute(tail, ("wide", "core"), [(i, i + 1) for i in range(time_count - 1)])
    spectrum = own + jnp.pad(earlier, ((0, 0), (0, spec_local - history), (0, 0)))
    flagged = (spectrum * flags.astype(jnp.float32).T[None]).astype(jnp.bfloat16)
    flagged = flagged.reshape(chan_count, 1, 2, spec_local, local_inputs)
    sent = jnp.broadcast_to(flagged, (chan_count, wide, 2, spec_local, local_inputs))
    sent = sent.reshape(chan_count * wide, 2, spec_local, local_inputs)
    mine = lax.all_to_all(sent, ("chan", "wide"), split_axis=0, concat_axis=0, tiled=True)
    other = lax.ppermute(mine, "core", [(0, 1), (1, 0)])
    shape = (chan_count, wide, 2, spec_local, local_inputs)
    mine, other = mine.reshape(shape), other.reshape(shape)
    scale = 1.0 / math.sqrt(spec_local * time_count)
    own_rows = inputs // time_count
    if aligned:
        return correlate((mine, other), offsets, scale, own_rows)[None]
    lanes = 256
    rows = [regroup(pieces, lanes) for pieces in (mine, other)]
    cols = [regroup(jnp.roll(pieces, -offsets[0], axis=0), lanes) for pieces in (mine, other)]
    return correlate((*rows, *cols), offsets * 0, scale, own_rows)[None]


def solution(mesh):
    devices = mesh.devices.reshape(mesh.shape["chan"], -1, 2)
    split = Mesh(devices, ("chan", "wide", "core"))
    time = ("wide", "core")
    in_specs = (P("chan", time), P(), P("chan", time), P("chan"))
    out_specs = P("chan", time, None, None)
    return jax.shard_map(shards, mesh=split, in_specs=in_specs, out_specs=out_specs, check_vma=False)
```
